256 devices in a mesh: dp: 16 (over x_hi, z), group: 16 (over x_lo, y, core).
Axes of the slice: x: 4 (x_hi: 2, x_lo: 2; x = x_hi * 2 + x_lo), y: 4, z: 8, core: 2. Of those that a mesh axis runs over, the one named last changes fastest.
Arguments:
- motion_frames: bfloat16 [65536, 256], P(('dp', 'group')), may hold values from -6 to 6
- enc_weight: bfloat16 [768, 2048], replicated, may hold values from -0.21875 to 0.21875
- code_ids: int32 [16, 32768], P('group', 'dp'), may hold values from 0 to 8191
- clip_offsets: int32 [256, 8], P(('dp', 'group')), may hold values from 0 to 127
- codebook: bfloat16 [16, 8192, 128], P('group'), may hold values from -6 to 6
- ema_sums: float32 [16, 8192, 128], P('group', 'dp'), may hold values from -18 to 18
- ema_counts: float32 [16, 8192], P('group', 'dp'), may hold values from 1 to 30
- dec_weight: bfloat16 [2048, 512], replicated, may hold values from -0.125 to 0.125
Outputs:
- decoded: bfloat16 [65536, 256], P(('dp', 'group'))
- commit_error: float32 [16, 32768], P('group', 'dp')
- new_codebook: float32 [16, 8192, 128], P('group', 'dp')
- new_counts: float32 [16, 8192], P('group', 'dp')
The draws below stay inside these ranges and needn't reach their ends.
Inputs may be any that keep to these rules, and one draw needn't show every extreme that they name: A clip begins at latent frame s * 128 + clip_offsets[s, k] of time block s; repeated offsets may occur.
All inputs are finite; a program needn't handle non-finite values.
Results may differ from the reference program's by a relative error of at most 0.0013.
Values may be sent and summed in bfloat16 or wider, within the bound.
No kernel may reach another device: no remote copies, remote signals or barrier semaphores. Data moves between devices by JAX's collectives and lax.ppermute only.
A program may use at most 64 MiB of HBM per device.

```python
import math
import jax
import jax.numpy as jnp
from jax import lax

FEAT = 256
LATENT = 2048
GROUPS = 16
CODES = 8192
L_DEV = 128
CLIP_DEV = 8
GROUP_CH = 128
SHARDS = 256
TL = 32768
FRAMES = 65536


def with_ends(entries, stream_key, smallest, high):
    place = [jax.random.randint(jax.random.fold_in(stream_key, axis), (), 0, length) for axis, length in enumerate(entries.shape)]
    widest = entries.shape.index(max(entries.shape))
    beside = place[:widest] + [(place[widest] + 1) % entries.shape[widest]] + place[widest + 1:]
    return entries.at[tuple(place)].set(smallest).at[tuple(beside)].set(high)


def level_of(own_key, dims, shards, low, high):
    factor_of, own = 1.0, jax.random.fold_in(own_key, 6)
    for position, parts in shards:
        steps = jnp.exp(jax.random.uniform(jax.random.fold_in(own, position), (parts,), jnp.float32, low / len(shards), high / len(shards)))
        factor_of = factor_of * jnp.repeat(steps, dims[position] // parts).reshape([-1 if axis == position else 1 for axis in range(len(dims))])
    return factor_of


def centred(own_key, extent, scale, limit, split=(), held_as=jnp.bfloat16):
    array = jax.random.normal(own_key, extent, jnp.float32) * scale
    if len(split) > 0:
        array = level_of(own_key, extent, split, -0.22, 0.18) * array
    return jnp.clip(array, min=-limit, max=limit).astype(held_as)


def setup_inputs(seed: int = 0) -> dict:
    arg_keys = jax.random.split(jax.random.key(seed), 9)
    return {
        "motion_frames": centred(arg_keys[0], (FRAMES, FEAT), 1.0, 6.0, ((0, 256),)),
        "enc_weight": centred(arg_keys[1], (3 * FEAT, LATENT), (3 * FEAT) ** -0.5, 0.21875),
        "code_ids": with_ends(jax.random.randint(arg_keys[2], (GROUPS, TL), 0, CODES), jax.random.fold_in(arg_keys[2], 1), 0, CODES - 1).astype(jnp.int32),
        "clip_offsets": with_ends(jax.random.randint(arg_keys[3], (SHARDS, CLIP_DEV), 0, L_DEV), jax.random.fold_in(arg_keys[3], 1), 0, L_DEV - 1).astype(jnp.int32),
        "codebook": centred(arg_keys[4], (GROUPS, CODES, GROUP_CH), 1.0, 6.0, ((0, 16),)),
        "ema_sums": centred(arg_keys[5], (GROUPS, CODES, GROUP_CH), 3.0, 18.0, ((0, 16), (1, 16)), jnp.float32),
        "ema_counts": jnp.clip(jnp.exp(math.log(30.0) - 3.4011974 * jax.random.uniform(arg_keys[6], (GROUPS, CODES), jnp.float32) ** level_of(arg_keys[6], (GROUPS, CODES), ((0, 16), (1, 16)), -0.2, 0.2)), 1.0, 30.0),
        "dec_weight": centred(arg_keys[7], (LATENT, 2 * FEAT), LATENT ** -0.5, 0.125),
    }


ema_decay = 0.9


def reference(motion_frames, enc_weight, code_ids, clip_offsets, codebook, ema_sums, ema_counts, dec_weight):
    total = motion_frames.shape[0] // 2
    feat = motion_frames.shape[1]
    pairs = motion_frames.reshape(total, 2, feat)
    even_rows = pairs[:, 0]
    odd_rows = pairs[:, 1]
    earlier = jnp.concatenate([jnp.zeros((1, feat), motion_frames.dtype), odd_rows[:-1]], axis=0)
    local = jnp.arange(L_DEV, dtype=jnp.int32)
    starts = jnp.any(local[None, :, None] == clip_offsets[:, None, :], axis=2).reshape(total, 1)
    earlier = jnp.where(starts, jnp.zeros_like(earlier), earlier)
    stacked = jnp.concatenate([earlier, even_rows, odd_rows], axis=1)
    width = GROUP_CH

    def one_group(carry, index):
        w_slice = lax.dynamic_slice_in_dim(enc_weight, index * width, width, 1)
        latent = jnp.dot(stacked, w_slice, preferred_element_type=jnp.float32).astype(jnp.bfloat16)
        ids = code_ids[index]
        picked = jnp.take(codebook[index], ids, axis=0)
        diff = latent.astype(jnp.float32) - picked.astype(jnp.float32)
        error = jnp.mean(diff * diff, axis=1)
        sums = jax.ops.segment_sum(latent.astype(jnp.float32), ids, num_segments=CODES)
        counts = jax.ops.segment_sum(jnp.ones((total,), jnp.float32), ids, num_segments=CODES)
        d_slice = lax.dynamic_slice_in_dim(dec_weight, index * width, width, 0)
        carry = carry + jnp.dot(picked, d_slice, preferred_element_type=jnp.float32)
        return carry, (error, sums, counts)

    init = jnp.zeros((total, dec_weight.shape[1]), jnp.float32)
    summed, outs = lax.scan(one_group, init, jnp.arange(GROUPS, dtype=jnp.int32))
    errors, sums, counts = outs
    new_counts = ema_decay * ema_counts + (1.0 - ema_decay) * counts
    new_codebook = (ema_decay * ema_sums + (1.0 - ema_decay) * sums) / new_counts[:, :, None]
    decoded = summed.astype(jnp.bfloat16).reshape(2 * total, feat)
    return decoded, errors, new_codebook, new_counts
```

```python
import functools

import jax
import jax.numpy as jnp
from jax import lax
from jax.experimental import pallas as pl
from jax.experimental.pallas import tpu as pltpu
from jax.sharding import PartitionSpec as P

ema_decay = 0.9

F32 = jnp.float32
BF16 = jnp.bfloat16
I32 = jnp.int32

LANES = 128
PARTS = 16
BLOCK = 192
CAP = 184
SHARE = 512

VMEM = pl.BlockSpec(memory_space=pltpu.VMEM)


def one_hot(condition):
    return jnp.where(condition, 1.0, 0.0).astype(BF16)


def iota(shape, axis):
    return lax.broadcasted_iota(I32, shape, axis)


def id_columns(ids_ref):
    rows = [ids_ref[0:1, c * LANES:(c + 1) * LANES] for c in range(PARTS)]
    return jnp.concatenate(rows, axis=0).T


def pick_kernel(ids_ref, book_ref, out_ref):
    columns = id_columns(ids_ref)
    lanes = iota((LANES, 1024), 1)
    step = 4
    for first in range(0, PARTS, step):
        ids = jnp.concatenate(
            [columns[:, c:c + 1] for c in range(first, first + step)], axis=0
        )
        low, top = ids & 1023, ids >> 10
        selector = jnp.concatenate(
            [one_hot(low[k * LANES:(k + 1) * LANES] == lanes) for k in range(step)], axis=0
        )
        picked = jnp.zeros((step * LANES, LANES), F32)
        for pair in range(4):
            begin = pair * 2048
            tile = jnp.concatenate(
                [book_ref[begin:begin + 1024, :], book_ref[begin + 1024:begin + 2048, :]], axis=1
            )
            both = jnp.dot(selector, tile, preferred_element_type=F32)
            picked = jnp.where(top == 2 * pair, both[:, :LANES], picked)
            picked = jnp.where(top == 2 * pair + 1, both[:, LANES:], picked)
        picked = picked.astype(BF16)
        for k in range(step):
            out_ref[first + k, LANES:, :] = picked[k * LANES:(k + 1) * LANES]


def encode_kernel(frames_ref, halo_ref, clips_ref, weight_ref, base_ref, out_ref):
    del base_ref
    frames = frames_ref[...]
    row, col = iota((LANES, 256), 0), iota((LANES, 256), 1)
    even = jnp.dot(one_hot(col == 2 * row), frames, preferred_element_type=F32)
    odd = jnp.dot(one_hot(col == 2 * row + 1), frames, preferred_element_type=F32)
    earlier = jnp.dot(one_hot(col == 2 * row - 1), frames, preferred_element_type=F32)
    earlier = jnp.where(row == 0, halo_ref[...].astype(F32), earlier)
    hits = jnp.where(iota((LANES, 8), 0) == clips_ref[...], 1.0, 0.0)
    starts = jnp.max(hits, axis=1, keepdims=True)
    earlier = jnp.where(starts > 0.0, 0.0, earlier)
    stacked = jnp.concatenate([earlier, even, odd], axis=1).astype(BF16)
    for pair in range(PARTS // 2):
        wide = jnp.dot(
            stacked, weight_ref[:, pair * 256:(pair + 1) * 256], preferred_element_type=F32
        ).astype(BF16)
        out_ref[2 * pair, :LANES, :] = wide[:, :LANES]
        out_ref[2 * pair + 1, :LANES, :] = wide[:, LANES:]


def route_kernel(round_ref, ids_ref, owned_ref, out_ref, total_ref):
    passed = round_ref[0, 0] * CAP
    dest_rows, tables = [], []
    sub16 = iota((PARTS, LANES), 0)
    for c in range(PARTS):
        dest = ids_ref[0:1, c * LANES:(c + 1) * LANES] >> 9
        dest_rows.append(dest)
        tables.append(jnp.where(sub16 == dest, 1.0, 0.0))
    upper = one_hot(iota((LANES, LANES), 0) <= iota((LANES, LANES), 1))
    cumulative = jnp.dot(
        jnp.concatenate(tables, axis=0).astype(BF16), upper, preferred_element_type=F32
    )
    offset = jnp.zeros((PARTS, 1), F32)
    place_rows = []
    for c in range(PARTS):
        inside = cumulative[c * PARTS:(c + 1) * PARTS]
        rank = jnp.sum(tables[c] * (inside + (offset - 1.0)), axis=0, keepdims=True)
        rank = rank.astype(I32) - passed
        kept = (rank >= 0) & (rank < CAP)
        place_rows.append(jnp.where(kept, (dest_rows[c] & 3) * BLOCK + rank, -1))
        offset = offset + inside[:, LANES - 1:]
    most = jnp.max(offset, axis=0, keepdims=True)
    need = jnp.ones((1, 1), F32)
    for k in range(1, 2048 // CAP + 1):
        need = need + jnp.where(most > float(k * CAP), 1.0, 0.0)

    columns = id_columns(ids_ref)
    lane = iota((LANES, LANES), 1)
    rows = iota((4 * BLOCK, LANES), 0)
    for pair in range(PARTS // 2):
        wides, selectors = [], []
        for c in (2 * pair, 2 * pair + 1):
            ids = columns[:, c:c + 1]
            quarter = ids >> 11
            code = ids & (SHARE - 1)
            latent = owned_ref[c, :LANES, :]
            zero = jnp.zeros_like(latent)
            pieces = [jnp.where(quarter == q, latent, zero) for q in range(4)]
            mark = jnp.where((lane & 1) == 1, code & 15, (code >> 4) + 1)
            mark = jnp.where((lane >> 3) == quarter, mark, 0)
            pieces.append(mark.astype(F32).astype(BF16))
            wides.append(jnp.concatenate(pieces, axis=1))
            selectors.append(one_hot(rows == place_rows[c]))
        part = jnp.dot(
            jnp.concatenate(selectors, axis=1), jnp.concatenate(wides, axis=0), preferred_element_type=F32
        )
        if pair == 0:
            total_ref[...] = part
        else:
            total_ref[...] += part

    row8 = iota((8, LANES), 0)
    for j in range(4):
        begin = j * BLOCK
        marks = total_ref[begin:begin + BLOCK, 512:640]
        first = marks[:LANES].T
        second = jnp.concatenate([marks[LANES:], jnp.zeros((2 * LANES - BLOCK, LANES), F32)], axis=0).T
        for q in range(4):
            meta = jnp.where(
                row8 < 2,
                first[8 * q:8 * q + 8],
                jnp.where(row8 < 4, second[8 * q:8 * q + 8], need),
            )
            data = total_ref[begin:begin + CAP, q * LANES:(q + 1) * LANES]
            out_ref[4 * q + j] = jnp.concatenate([data, meta], axis=0).astype(BF16)


def update_kernel(
    message_ref, held_ref, ema_sums_ref, ema_counts_ref, book_ref, counts_ref, kept_ref, need_ref
):
    codes = iota((SHARE, LANES), 0).astype(F32)
    ones = jnp.ones((2 * LANES, LANES), BF16)
    kept_ref[...] = held_ref[...]
    need = jnp.zeros((1, 1), F32)
    tails = []
    selectors, datas = [], []

    def flush():
        data = jnp.concatenate(datas, axis=0)
        kept_ref[...] += jnp.dot(
            jnp.concatenate(selectors, axis=1),
            jnp.concatenate([data, ones], axis=1),
            preferred_element_type=F32,
        )
        selectors.clear()
        datas.clear()

    for s in range(PARTS):
        meta = message_ref[s, BLOCK - 16:, :].astype(F32)[8:]
        code = (meta[0:1] - 1.0) * 16.0 + meta[1:2]
        need = jnp.maximum(need, meta[4:5, 0:1])
        tails.append((meta[2:3], meta[3:4]))
        selectors.append(one_hot(codes == code))
        datas.append(message_ref[s, :LANES, :])
        if len(datas) == 2:
            flush()
    for s in range(0, PARTS, 2):
        (high0, low0), (high1, low1) = tails[s], tails[s + 1]
        shift = 2 * LANES - BLOCK
        high = high0 + pltpu.roll(jnp.broadcast_to(high1, (8, LANES)), shift, 1)[0:1]
        low = low0 + pltpu.roll(jnp.broadcast_to(low1, (8, LANES)), shift, 1)[0:1]
        selectors.append(one_hot(codes == (high - 1.0) * 16.0 + low))
        datas.append(
            jnp.concatenate([message_ref[s, LANES:, :], message_ref[s + 1, LANES:, :]], axis=0)
        )
        if len(datas) == 2:
            flush()
    need_ref[0, 0] = jnp.max(need).astype(I32)
    diagonal = iota((LANES, LANES), 0) == iota((LANES, LANES), 1)
    for k in range(SHARE // LANES):
        begin = k * LANES
        old = jnp.broadcast_to(ema_counts_ref[0:1, begin:begin + LANES], (LANES, LANES)).T
        sums, counts = kept_ref[begin:begin + LANES, :LANES], kept_ref[begin:begin + LANES, LANES:]
        new_counts = ema_decay * old + (1.0 - ema_decay) * counts
        book_ref[begin:begin + LANES, :] = (
            ema_decay * ema_sums_ref[begin:begin + LANES, :] + (1.0 - ema_decay) * sums
        ) / new_counts
        counts_ref[0:1, begin:begin + LANES] = jnp.sum(
            jnp.where(diagonal, new_counts, 0.0), axis=0, keepdims=True
        )


def decode_kernel(got_ref, sent_ref, weight_ref, out_ref, error_ref):
    picked = jnp.concatenate([got_ref[g, LANES:, :] for g in range(PARTS)], axis=1)
    decoded = jnp.dot(picked, weight_ref[...], preferred_element_type=F32).astype(BF16)
    halves = jnp.concatenate([decoded[:, :256], decoded[:, 256:]], axis=0)
    row, col = iota((256, 256), 0), iota((256, 256), 1)
    source = (row >> 1) + (row & 1) * LANES
    out_ref[...] = jnp.dot(one_hot(col == source), halves, preferred_element_type=F32).astype(BF16)
    for c in range(PARTS):
        diff = got_ref[c, :LANES, :].astype(F32) - sent_ref[c, LANES:, :].astype(F32)
        error = jnp.sum((diff * diff).T, axis=0, keepdims=True) * (1.0 / LANES)
        error_ref[0:1, c * LANES:(c + 1) * LANES] = error


def call(kernel, out_shape, count, flops, size, scalars=0, scalar_out=False, scratch=(), aliases=None):
    in_specs = [pl.BlockSpec(memory_space=pltpu.SMEM)] * scalars + [VMEM] * (count - scalars)
    out_specs = jax.tree.map(lambda _: VMEM, out_shape)
    if scalar_out:
        out_specs = out_specs[:-1] + (pl.BlockSpec(memory_space=pltpu.SMEM),)
    return pl.pallas_call(
        kernel,
        out_shape=out_shape,
        in_specs=in_specs,
        out_specs=out_specs,
        scratch_shapes=list(scratch),
        input_output_aliases=aliases or {},
        cost_estimate=pl.CostEstimate(flops=flops, bytes_accessed=size, transcendentals=0),
        compiler_params=pltpu.CompilerParams(vmem_limit_bytes=40 << 20),
    )


def passed_along(shard, axis, by):
    size = lax.axis_size(axis)
    pairs = [(i, i + by) for i in range(size) if 0 <= i + by < size]
    return lax.ppermute(shard, axis, pairs)


def body(
    motion_frames, enc_weight, code_ids, clip_offsets, codebook, ema_sums, ema_counts, dec_weight
):
    shape = jax.ShapeDtypeStruct
    halo = passed_along(motion_frames[-1:], ("dp", "group"), 1)
    buffer = shape((PARTS, 2 * LANES, LANES), BF16)
    picked = call(pick_kernel, buffer, 2, 4 << 30, 4 << 20)(code_ids, codebook[0])
    sent = call(encode_kernel, buffer, 5, 400 << 20, 4 << 20, aliases={4: 0})(
        motion_frames, halo, clip_offsets, enc_weight, picked
    )
    got = lax.all_to_all(sent, "group", split_axis=0, concat_axis=0)

    def one_round(index, held):
        message = call(
            route_kernel, shape((PARTS, BLOCK, LANES), BF16), 3, 2 << 30, 2 << 20, scalars=1,
            scratch=[pltpu.VMEM((4 * BLOCK, 5 * LANES), F32)],
        )(index.reshape(1, 1), code_ids, got)
        arrived = lax.all_to_all(message, "dp", split_axis=0, concat_axis=0)
        return call(
            update_kernel,
            (
                shape((SHARE, LANES), F32),
                shape((1, SHARE), F32),
                shape((SHARE, 2 * LANES), F32),
                shape((1, 1), I32),
            ),
            4, 800 << 20, 2 << 20, scalar_out=True,
        )(arrived, held, ema_sums[0], ema_counts)

    decoded, commit_error = call(
        decode_kernel,
        (shape((256, 256), BF16), shape((1, PARTS * LANES), F32)),
        3, 300 << 20, 4 << 20,
    )(got, sent, dec_weight)

    first = one_round(jnp.zeros((), I32), jnp.zeros((SHARE, 2 * LANES), F32))

    def more(state):
        return state[0] < state[4][0, 0]

    def again(state):
        index, _, _, held, _ = state
        return (index + 1, *one_round(index, held))

    _, new_codebook, new_counts, _, _ = lax.while_loop(more, again, (jnp.ones((), I32), *first))
    return (decoded, commit_error, new_codebook[None], new_counts)


def solution(mesh):
    return jax.shard_map(
        body,
        mesh=mesh,
        in_specs=(
            P(("dp", "group"), None),
            P(),
            P("group", "dp"),
            P(("dp", "group"), None),
            P("group", None, None),
            P("group", "dp", None),
            P("group", "dp"),
            P(),
        ),
        out_specs=(
            P(("dp", "group"), None),
            P("group", "dp"),
            P("group", "dp", None),
            P("group", "dp"),
        ),
        check_vma=False,
    )
```

```python
import functools

import jax
import jax.numpy as jnp
from jax import lax
from jax.experimental import pallas as pl
from jax.experimental.pallas import tpu as pltpu
from jax.sharding import PartitionSpec as P

ema_decay = 0.9

F32 = jnp.float32
BF16 = jnp.bfloat16
I32 = jnp.int32

LANES = 128
PARTS = 16
BLOCK = 192
CAP = 184
SHARE = 512

VMEM = pl.BlockSpec(memory_space=pltpu.VMEM)
IN_HBM = pl.BlockSpec(memory_space=pltpu.HBM)


def one_hot(condition):
    return jnp.where(condition, 1.0, 0.0).astype(BF16)


def iota(shape, axis):
    return lax.broadcasted_iota(I32, shape, axis)


def id_columns(ids_ref):
    rows = [ids_ref[0:1, c * LANES:(c + 1) * LANES] for c in range(PARTS)]
    return jnp.concatenate(rows, axis=0).T


def relative_blocks(place_ref):
    x, y, core = place_ref[0], place_ref[1], place_ref[2]
    return [
        ((x ^ dx) * 4 + ((y + dy) & 3)) * 2 + (core ^ dc)
        for dx in range(2) for dc in range(2) for dy in range(4)
    ]


def pick_kernel(place_ref, ids_ref, book_ref, near_ref, far_ref, beside_ref):
    blocks = relative_blocks(place_ref)
    rows = [ids_ref[0:1, pl.ds(pl.multiple_of(b * LANES, LANES), LANES)] for b in blocks]
    columns = jnp.concatenate(rows, axis=0).T
    lanes = iota((LANES, 1024), 1)
    step = 4
    for first in range(0, PARTS, step):
        ids = jnp.concatenate(
            [columns[:, c:c + 1] for c in range(first, first + step)], axis=0
        )
        low, top = ids & 1023, ids >> 10
        selector = jnp.concatenate(
            [one_hot(low[k * LANES:(k + 1) * LANES] == lanes) for k in range(step)], axis=0
        )
        picked = jnp.zeros((step * LANES, LANES), F32)
        for pair in range(4):
            begin = pair * 2048
            tile = jnp.concatenate(
                [book_ref[begin:begin + 1024, :], book_ref[begin + 1024:begin + 2048, :]], axis=1
            )
            both = jnp.dot(selector, tile, preferred_element_type=F32)
            picked = jnp.where(top == 2 * pair, both[:, :LANES], picked)
            picked = jnp.where(top == 2 * pair + 1, both[:, LANES:], picked)
        picked = picked.astype(BF16)
        for k in range(step):
            out_ref = (near_ref, far_ref, beside_ref)[min(first // 4, 2)]
            out_ref[(first + k) % (4 if first < 8 else 8)] = picked[k * LANES:(k + 1) * LANES]


def encode_kernel(
    frames_ref, clips_ref, weight_hbm, out_ref, head_ref, first_ref, weight_ref, stage_ref, in_sems, sems
):
    def strip(pair):
        columns = pl.ds(pair * 256, 256)
        return pltpu.make_async_copy(
            weight_hbm.at[:, columns], weight_ref.at[:, columns], in_sems.at[pair]
        )

    for pair in range(PARTS // 2):
        strip(pair).start()
    frames = frames_ref[...]
    row, col = iota((LANES, 256), 0), iota((LANES, 256), 1)
    even = jnp.dot(one_hot(col == 2 * row), frames, preferred_element_type=F32)
    odd = jnp.dot(one_hot(col == 2 * row + 1), frames, preferred_element_type=F32)
    earlier = jnp.dot(one_hot(col == 2 * row - 1), frames, preferred_element_type=F32)
    hits = jnp.where(iota((LANES, 8), 0) == clips_ref[...], 1.0, 0.0)
    starts = jnp.max(hits, axis=1, keepdims=True)
    earlier = jnp.where(starts > 0.0, 0.0, earlier)
    stacked = jnp.concatenate([earlier, even, odd], axis=1).astype(BF16)
    for pair in range(PARTS // 2):
        strip(pair).wait()
        wide = jnp.dot(
            stacked, weight_ref[:, pair * 256:(pair + 1) * 256], preferred_element_type=F32
        )
        first_ref[:, pair * 256:(pair + 1) * 256] = wide[:1]
        wide = wide.astype(BF16)
        for g, block in ((2 * pair, wide[:, :LANES]), (2 * pair + 1, wide[:, LANES:])):
            stage_ref[g] = block
            head_ref[g] = block[:16]
            pltpu.make_async_copy(stage_ref.at[g], out_ref.at[g], sems.at[g]).start()
    for g in range(PARTS):
        pltpu.make_async_copy(stage_ref.at[g], out_ref.at[g], sems.at[g]).wait()


def halo_kernel(
    halo_ref, clips_ref, head_ref, first_ref, weight_hbm, sent_ref, out_ref, weight_ref, stage_ref, in_sem, sem
):
    del sent_ref
    loaded = pltpu.make_async_copy(weight_hbm.at[pl.ds(0, 256), :], weight_ref, in_sem)
    loaded.start()
    starts = jnp.max(jnp.where(clips_ref[...] == 0, 1.0, 0.0), axis=1, keepdims=True)
    halo = jnp.where(starts > 0.0, 0.0, halo_ref[...].astype(F32))
    halo = jnp.broadcast_to(halo, (16, 256)).astype(BF16)
    loaded.wait()
    added = jnp.dot(halo, weight_ref[...], preferred_element_type=F32)
    whole = (added + first_ref[...]).astype(BF16)
    row = iota((16, LANES), 0)
    for g in range(PARTS):
        stage_ref[g] = jnp.where(row == 0, whole[:, g * LANES:(g + 1) * LANES], head_ref[g])
    copy = pltpu.make_async_copy(stage_ref, out_ref.at[:, pl.ds(0, 16), :], sem)
    copy.start()
    copy.wait()


def route_kernel(
    round_ref, ids_ref, got_ref, out_ref, total_ref, owned_ref, stage_ref, sems, got_sem
):
    loaded = pltpu.make_async_copy(got_ref, owned_ref, got_sem)
    loaded.start()
    passed = round_ref[0, 0] * CAP
    dest_rows, tables = [], []
    sub16 = iota((PARTS, LANES), 0)
    for c in range(PARTS):
        dest = ids_ref[0:1, c * LANES:(c + 1) * LANES] >> 9
        dest_rows.append(dest)
        tables.append(jnp.where(sub16 == dest, 1.0, 0.0))
    upper = one_hot(iota((LANES, LANES), 0) <= iota((LANES, LANES), 1))
    cumulative = jnp.dot(
        jnp.concatenate(tables, axis=0).astype(BF16), upper, preferred_element_type=F32
    )
    offset = jnp.zeros((PARTS, 1), F32)
    place_rows = []
    for c in range(PARTS):
        inside = cumulative[c * PARTS:(c + 1) * PARTS]
        rank = jnp.sum(tables[c] * (inside + (offset - 1.0)), axis=0, keepdims=True)
        rank = rank.astype(I32) - passed
        kept = (rank >= 0) & (rank < CAP)
        place_rows.append(jnp.where(kept, (dest_rows[c] & 3) * BLOCK + rank, -1))
        offset = offset + inside[:, LANES - 1:]
    most = jnp.max(offset, axis=0, keepdims=True)
    need = jnp.ones((1, 1), F32)
    for k in range(1, 2048 // CAP + 1):
        need = need + jnp.where(most > float(k * CAP), 1.0, 0.0)

    columns = id_columns(ids_ref)
    lane = iota((LANES, LANES), 1)
    rows = iota((4 * BLOCK, LANES), 0)
    loaded.wait()
    for pair in range(PARTS // 2):
        wides, selectors = [], []
        for c in (2 * pair, 2 * pair + 1):
            ids = columns[:, c:c + 1]
            quarter = ids >> 11
            code = ids & (SHARE - 1)
            latent = owned_ref[c]
            zero = jnp.zeros_like(latent)
            pieces = [jnp.where(quarter == q, latent, zero) for q in range(4)]
            mark = jnp.where((lane & 1) == 1, code & 15, (code >> 4) + 1)
            mark = jnp.where((lane >> 3) == quarter, mark, 0)
            pieces.append(mark.astype(F32).astype(BF16))
            wides.append(jnp.concatenate(pieces, axis=1))
            selectors.append(one_hot(rows == place_rows[c]))
        part = jnp.dot(
            jnp.concatenate(selectors, axis=1), jnp.concatenate(wides, axis=0), preferred_element_type=F32
        )
        if pair == 0:
            total_ref[...] = part
        else:
            total_ref[...] += part

    row8 = iota((8, LANES), 0)
    for j in range(4):
        begin = j * BLOCK
        marks = total_ref[begin:begin + BLOCK, 512:640]
        first = marks[:LANES].T
        second = jnp.concatenate([marks[LANES:], jnp.zeros((2 * LANES - BLOCK, LANES), F32)], axis=0).T
        for q in range(4):
            meta = jnp.where(
                row8 < 2,
                first[8 * q:8 * q + 8],
                jnp.where(row8 < 4, second[8 * q:8 * q + 8], need),
            )
            data = total_ref[begin:begin + CAP, q * LANES:(q + 1) * LANES]
            to = 4 * q + j
            stage_ref[to] = jnp.concatenate([data, meta], axis=0).astype(BF16)
            pltpu.make_async_copy(stage_ref.at[to], out_ref.at[to], sems.at[to]).start()
    for to in range(PARTS):
        pltpu.make_async_copy(stage_ref.at[to], out_ref.at[to], sems.at[to]).wait()


def update_kernel(
    message_ref, held_ref, ema_sums_ref, ema_counts_ref, book_ref, counts_ref, kept_ref, need_ref
):
    codes = iota((SHARE, LANES), 0).astype(F32)
    ones = jnp.ones((2 * LANES, LANES), BF16)
    kept_ref[...] = held_ref[...]
    need = jnp.zeros((1, 1), F32)
    tails = []
    selectors, datas = [], []

    def flush():
        data = jnp.concatenate(datas, axis=0)
        kept_ref[...] += jnp.dot(
            jnp.concatenate(selectors, axis=1),
            jnp.concatenate([data, ones], axis=1),
            preferred_element_type=F32,
        )
        selectors.clear()
        datas.clear()

    for s in range(PARTS):
        meta = message_ref[s, BLOCK - 16:, :].astype(F32)[8:]
        code = (meta[0:1] - 1.0) * 16.0 + meta[1:2]
        need = jnp.maximum(need, meta[4:5, 0:1])
        tails.append((meta[2:3], meta[3:4]))
        selectors.append(one_hot(codes == code))
        datas.append(message_ref[s, :LANES, :])
        if len(datas) == 2:
            flush()
    for s in range(0, PARTS, 2):
        (high0, low0), (high1, low1) = tails[s], tails[s + 1]
        shift = 2 * LANES - BLOCK
        high = high0 + pltpu.roll(jnp.broadcast_to(high1, (8, LANES)), shift, 1)[0:1]
        low = low0 + pltpu.roll(jnp.broadcast_to(low1, (8, LANES)), shift, 1)[0:1]
        selectors.append(one_hot(codes == (high - 1.0) * 16.0 + low))
        datas.append(
            jnp.concatenate([message_ref[s, LANES:, :], message_ref[s + 1, LANES:, :]], axis=0)
        )
        if len(datas) == 2:
            flush()
    need_ref[0, 0] = jnp.max(need).astype(I32)
    diagonal = iota((LANES, LANES), 0) == iota((LANES, LANES), 1)
    for k in range(SHARE // LANES):
        begin = k * LANES
        old = jnp.broadcast_to(ema_counts_ref[0:1, begin:begin + LANES], (LANES, LANES)).T
        sums, counts = kept_ref[begin:begin + LANES, :LANES], kept_ref[begin:begin + LANES, LANES:]
        new_counts = ema_decay * old + (1.0 - ema_decay) * counts
        book_ref[begin:begin + LANES, :] = (
            ema_decay * ema_sums_ref[begin:begin + LANES, :] + (1.0 - ema_decay) * sums
        ) / new_counts
        counts_ref[0:1, begin:begin + LANES] = jnp.sum(
            jnp.where(diagonal, new_counts, 0.0), axis=0, keepdims=True
        )


def gather_kernel(near_ref, far_ref, beside_ref, across_ref, *out_refs):
    for k, ref in enumerate((near_ref, far_ref, beside_ref, across_ref)):
        for dy in range(1, 4):
            out_refs[dy - 1][k] = ref[dy]


def decode_kernel(
    place_ref, near_ref, far_ref, beside_ref, across_ref, y1_ref, y2_ref, y3_ref, weight_ref, out_ref
):
    groups = relative_blocks(place_ref)
    slabs, weights = [], []
    for dy in range(4):
        for k, ref in enumerate((near_ref, far_ref, beside_ref, across_ref)):
            group = groups[4 * k + (4 - dy) % 4]
            slabs.append(ref[0] if dy == 0 else (y1_ref, y2_ref, y3_ref)[dy - 1][k])
            weights.append(weight_ref[pl.ds(pl.multiple_of(group * LANES, LANES), LANES), :])
    decoded = jnp.dot(
        jnp.concatenate(slabs, axis=1), jnp.concatenate(weights, axis=0), preferred_element_type=F32
    ).astype(BF16)
    halves = jnp.concatenate([decoded[:, :256], decoded[:, 256:]], axis=0)
    row, col = iota((256, 256), 0), iota((256, 256), 1)
    source = (row >> 1) + (row & 1) * LANES
    out_ref[...] = jnp.dot(one_hot(col == source), halves, preferred_element_type=F32).astype(BF16)


def error_kernel(place_ref, got_ref, near_ref, far_ref, beside_ref, error_ref):
    for k, block in enumerate(relative_blocks(place_ref)):
        picked = (near_ref, far_ref)[k // 4][k % 4] if k < 8 else beside_ref[k - 8]
        diff = got_ref[block].astype(F32) - picked.astype(F32)
        error = jnp.sum((diff * diff).T, axis=0, keepdims=True) * (1.0 / LANES)
        error_ref[0:1, pl.ds(pl.multiple_of(block * LANES, LANES), LANES)] = error


def call(kernel, out_shape, count, flops, size, scalars=0, hbm_in=0, out_specs=None, scratch=(), aliases=None, limit=40):
    in_specs = [pl.BlockSpec(memory_space=pltpu.SMEM)] * scalars + [VMEM] * (count - scalars)
    in_specs[count - hbm_in:] = [IN_HBM] * hbm_in
    return pl.pallas_call(
        kernel,
        out_shape=out_shape,
        in_specs=in_specs,
        out_specs=out_specs or jax.tree.map(lambda _: VMEM, out_shape),
        scratch_shapes=list(scratch),
        input_output_aliases=aliases or {},
        cost_estimate=pl.CostEstimate(flops=flops, bytes_accessed=size, transcendentals=0),
        compiler_params=pltpu.CompilerParams(vmem_limit_bytes=limit << 20),
    )


def passed_along(shard, axis, by):
    size = lax.axis_size(axis)
    pairs = [(i, i + by) for i in range(size) if 0 <= i + by < size]
    return lax.ppermute(shard, axis, pairs)


def moved(shard, dx, dy, dc):
    pairs = [
        ((x * 4 + y) * 2 + c, ((x ^ dx) * 4 + (y + dy) % 4) * 2 + (c ^ dc))
        for x in range(2) for y in range(4) for c in range(2)
    ]
    return lax.ppermute(shard, "group", pairs)


def body(
    motion_frames, enc_weight, code_ids, clip_offsets, codebook, ema_sums, ema_counts, dec_weight
):
    shape = jax.ShapeDtypeStruct
    me = lax.axis_index("group").astype(I32)
    place = jnp.stack([me >> 3, (me >> 1) & 3, me & 1])
    halo = passed_along(motion_frames[-1:], ("dp", "group"), 1)
    blocks = shape((PARTS, LANES, LANES), BF16)
    four, eight = shape((4, LANES, LANES), BF16), shape((8, LANES, LANES), BF16)
    started, head, row = call(
        encode_kernel,
        (blocks, shape((PARTS, 16, LANES), BF16), shape((1, PARTS * LANES), F32)),
        3, 400 << 20, 4 << 20, hbm_in=1, limit=60,
        out_specs=(IN_HBM, VMEM, VMEM),
        scratch=[
            pltpu.VMEM(enc_weight.shape, BF16),
            pltpu.VMEM(blocks.shape, BF16),
            pltpu.SemaphoreType.DMA((PARTS // 2,)),
            pltpu.SemaphoreType.DMA((PARTS,)),
        ],
    )(motion_frames, clip_offsets, enc_weight)
    sent = call(
        halo_kernel, blocks, 6, 20 << 20, 1 << 20, hbm_in=2, limit=60, out_specs=IN_HBM, aliases={5: 0},
        scratch=[
            pltpu.VMEM((256, enc_weight.shape[1]), BF16),
            pltpu.VMEM((PARTS, 16, LANES), BF16),
            pltpu.SemaphoreType.DMA,
            pltpu.SemaphoreType.DMA,
        ],
    )(halo, clip_offsets, head, row, enc_weight, started)
    sent, late_ids = lax.optimization_barrier((sent, code_ids))
    near, far, beside = call(pick_kernel, (four, four, eight), 3, 4 << 30, 4 << 20, scalars=1)(
        place, late_ids, codebook[0]
    )
    got = lax.all_to_all(sent, "group", split_axis=0, concat_axis=0)
    commit_error = call(
        error_kernel, shape((1, PARTS * LANES), F32), 5, 1 << 20, 1 << 20, scalars=1
    )(place, got, near, far, beside)

    from_x = moved(beside, 1, 0, 0)
    from_core = moved(far, 0, 0, 1)

    def route(index):
        message = shape((PARTS, BLOCK, LANES), BF16)
        return call(
            route_kernel, message, 3, 2 << 30, 2 << 20, scalars=1, hbm_in=1, out_specs=IN_HBM, limit=60,
            scratch=[
                pltpu.VMEM((4 * BLOCK, 5 * LANES), F32),
                pltpu.VMEM(blocks.shape, BF16),
                pltpu.VMEM(message.shape, BF16),
                pltpu.SemaphoreType.DMA((PARTS,)),
                pltpu.SemaphoreType.DMA,
            ],
        )(index.reshape(1, 1), code_ids, got)

    def one_round(message, held):
        arrived = lax.all_to_all(message, "dp", split_axis=0, concat_axis=0)
        return call(
            update_kernel,
            (
                shape((SHARE, LANES), F32),
                shape((1, SHARE), F32),
                shape((SHARE, 2 * LANES), F32),
                shape((1, 1), I32),
            ),
            4, 800 << 20, 2 << 20,
            out_specs=(VMEM, VMEM, VMEM, pl.BlockSpec(memory_space=pltpu.SMEM)),
        )(arrived, held, ema_sums[0], ema_counts)

    message, from_x, from_core = lax.optimization_barrier((route(jnp.zeros((), I32)), from_x, from_core))
    across = moved(from_x[4:], 0, 0, 1)
    columns = call(gather_kernel, (four,) * 3, 4, 1 << 20, 1 << 20)(near, from_core, from_x, across)
    columns = [moved(columns[dy - 1], 0, dy, 0) for dy in range(1, 4)]
    decoded = call(decode_kernel, shape((256, 256), BF16), 9, 300 << 20, 4 << 20, scalars=1)(
        place, near, from_core, from_x, across, *columns, dec_weight
    )

    first = one_round(message, jnp.zeros((SHARE, 2 * LANES), F32))

    def more(state):
        return state[0] < state[4][0, 0]

    def again(state):
        index, _, _, held, _ = state
        return (index + 1, *one_round(route(index), held))

    _, new_codebook, new_counts, _, _ = lax.while_loop(more, again, (jnp.ones((), I32), *first))
    return (decoded, commit_error, new_codebook[None], new_counts)


def solution(mesh):
    return jax.shard_map(
        body,
        mesh=mesh,
        in_specs=(
            P(("dp", "group"), None),
            P(),
            P("group", "dp"),
            P(("dp", "group"), None),
            P("group", None, None),
            P("group", "dp", None),
            P("group", "dp"),
            P(),
        ),
        out_specs=(
            P(("dp", "group"), None),
            P("group", "dp"),
            P("group", "dp", None),
            P("group", "dp"),
        ),
        check_vma=False,
    )
```

```python
import jax
import jax.numpy as jnp
from jax import lax
from jax.experimental import pallas as pl
from jax.experimental.pallas import tpu as pltpu
from jax.sharding import PartitionSpec as P

ema_decay = 0.9

F32 = jnp.float32
BF16 = jnp.bfloat16
I32 = jnp.int32

LANES = 128
PARTS = 16
BLOCK = 192
CAP = 184
SHARE = 512
NEED = 56
TALL = 144

VMEM = pl.BlockSpec(memory_space=pltpu.VMEM)
IN_HBM = pl.BlockSpec(memory_space=pltpu.HBM)


def one_hot(condition):
    return jnp.where(condition, 1.0, 0.0).astype(BF16)


def iota(shape, axis):
    return lax.broadcasted_iota(I32, shape, axis)


def id_columns(ids_ref):
    rows = [ids_ref[0:1, c * LANES:(c + 1) * LANES] for c in range(PARTS)]
    return jnp.concatenate(rows, axis=0).T


def relative_blocks(place_ref):
    x, y, core = place_ref[0], place_ref[1], place_ref[2]
    return [
        ((x ^ dx) * 4 + ((y + dy) & 3)) * 2 + (core ^ dc)
        for dx in range(2) for dc in range(2) for dy in range(4)
    ]


def pick_kernel(place_ref, ids_ref, book_ref, near_ref, far_ref, beside_ref):
    blocks = relative_blocks(place_ref)
    rows = [ids_ref[0:1, pl.ds(pl.multiple_of(b * LANES, LANES), LANES)] for b in blocks]
    columns = jnp.concatenate(rows, axis=0).T
    lanes = iota((LANES, 1024), 1)
    step = 4
    for first in range(0, PARTS, step):
        ids = jnp.concatenate(
            [columns[:, c:c + 1] for c in range(first, first + step)], axis=0
        )
        low, top = ids & 1023, ids >> 10
        selector = jnp.concatenate(
            [one_hot(low[k * LANES:(k + 1) * LANES] == lanes) for k in range(step)], axis=0
        )
        picked = jnp.zeros((step * LANES, LANES), F32)
        for pair in range(4):
            begin = pair * 2048
            tile = jnp.concatenate(
                [book_ref[begin:begin + 1024, :], book_ref[begin + 1024:begin + 2048, :]], axis=1
            )
            both = jnp.dot(selector, tile, preferred_element_type=F32)
            picked = jnp.where(top == 2 * pair, both[:, :LANES], picked)
            picked = jnp.where(top == 2 * pair + 1, both[:, LANES:], picked)
        picked = picked.astype(BF16)
        for k in range(step):
            out_ref = (near_ref, far_ref, beside_ref)[min(first // 4, 2)]
            out_ref[(first + k) % (4 if first < 8 else 8)] = picked[k * LANES:(k + 1) * LANES]


def split3(values):
    first = values.astype(BF16).astype(F32)
    second = (values - first).astype(BF16).astype(F32)
    return first, second, values - first - second


def stacked_rows(rows, shape):
    row, table = iota(shape, 0), jnp.zeros(shape, F32)
    for k, values in enumerate(rows):
        table = jnp.where(row == k, values, table)
    return table


def encode_kernel(
    frames_hbm, clips_hbm, weight_hbm, out_ref, frames_ref, clips_ref, weight_ref, stage_ref, in_sems, sems
):
    loads = [
        pltpu.make_async_copy(frames_hbm, frames_ref, in_sems.at[6]),
        pltpu.make_async_copy(clips_hbm, clips_ref, in_sems.at[7]),
    ]
    for k in range(6):
        rows = pl.ds(k * LANES, LANES)
        loads.append(
            pltpu.make_async_copy(weight_hbm.at[rows, :], weight_ref.at[rows, :], in_sems.at[k])
        )
    for load in loads:
        load.start()
    loads[0].wait()
    loads[1].wait()
    frames = frames_ref[...]
    row, col = iota((LANES, 256), 0), iota((LANES, 256), 1)
    even = jnp.dot(one_hot(col == 2 * row), frames, preferred_element_type=F32)
    odd = jnp.dot(one_hot(col == 2 * row + 1), frames, preferred_element_type=F32)
    earlier = jnp.dot(one_hot(col == 2 * row - 1), frames, preferred_element_type=F32)
    hits = jnp.where(iota((LANES, 8), 0) == clips_ref[...], 1.0, 0.0)
    starts = jnp.max(hits, axis=1, keepdims=True)
    earlier = jnp.where(starts > 0.0, 0.0, earlier)
    stacked = jnp.concatenate([earlier, even, odd], axis=1).astype(BF16)
    last = odd[LANES - 1:]
    for load in loads[2:]:
        load.wait()
    for pair in range(PARTS // 2):
        wide = jnp.dot(
            stacked, weight_ref[:, pair * 256:(pair + 1) * 256], preferred_element_type=F32
        )
        for g, block in ((2 * pair, wide[:, :LANES]), (2 * pair + 1, wide[:, LANES:])):
            extra = [last[:, :LANES], last[:, LANES:], *split3(block[:1]), starts[:1]]
            stage_ref[g, :LANES, :] = block.astype(BF16)
            stage_ref[g, LANES:, :] = stacked_rows(extra, (16, LANES)).astype(BF16)
            pltpu.make_async_copy(stage_ref.at[g], out_ref.at[g], sems.at[g]).start()
    for g in range(PARTS):
        pltpu.make_async_copy(stage_ref.at[g], out_ref.at[g], sems.at[g]).wait()


def finished_rows(lasts, parts, flags, weight):
    halo = jnp.concatenate(
        [jnp.concatenate(half, axis=0) for half in lasts], axis=1
    ).astype(BF16)
    added = jnp.dot(halo, weight, preferred_element_type=F32)
    added = jnp.where(jnp.concatenate(flags, axis=0) > 0.0, 0.0, added)
    return (added + jnp.concatenate(parts, axis=0)).astype(BF16).astype(F32)


def select_kernel(round_ref, ids_ref, place_ref, meta_ref):
    passed = round_ref[0, 0] * CAP
    dest_rows, tables = [], []
    sub16 = iota((PARTS, LANES), 0)
    for c in range(PARTS):
        dest = ids_ref[0:1, c * LANES:(c + 1) * LANES] >> 9
        dest_rows.append(dest)
        table = jnp.where(sub16 == dest, 1.0, 0.0)
        if c == 0:
            table = jnp.where(iota((PARTS, LANES), 1) == 0, 0.0, table)
        tables.append(table)
    upper = one_hot(iota((LANES, LANES), 0) <= iota((LANES, LANES), 1))
    cumulative = jnp.dot(
        jnp.concatenate(tables, axis=0).astype(BF16), upper, preferred_element_type=F32
    )
    offset = jnp.zeros((PARTS, 1), F32)
    rows = iota((4 * BLOCK, LANES), 0)
    selectors = []
    for c in range(PARTS):
        inside = cumulative[c * PARTS:(c + 1) * PARTS]
        rank = jnp.sum(tables[c] * (inside + (offset - 1.0)), axis=0, keepdims=True)
        rank = rank.astype(I32) - passed
        kept = (rank >= 0) & (rank < CAP)
        if c == 0:
            kept = kept & (iota((1, LANES), 1) > 0)
        place = jnp.where(kept, (dest_rows[c] & 3) * BLOCK + rank, -1)
        place_ref[:, c * LANES:(c + 1) * LANES] = place
        selectors.append(one_hot(rows == place))
        offset = offset + inside[:, LANES - 1:]
    most = jnp.max(offset, axis=0, keepdims=True)
    need = jnp.ones((1, 1), F32)
    for k in range(1, 2048 // CAP + 1):
        need = need + jnp.where(most > float(k * CAP), 1.0, 0.0)

    columns = id_columns(ids_ref)
    lane = iota((LANES, LANES), 1)
    pieces = []
    for c in range(PARTS):
        ids = columns[:, c:c + 1]
        code = ids & (SHARE - 1)
        mark = jnp.where((lane & 1) == 1, code & 15, (code >> 4) + 1)
        pieces.append(jnp.where((lane >> 3) == (ids >> 11), mark, 0).astype(F32).astype(BF16))
    marks = jnp.dot(
        jnp.concatenate(selectors, axis=1), jnp.concatenate(pieces, axis=0), preferred_element_type=F32
    )
    lane8, row8 = iota((8, LANES), 1), iota((8, LANES), 0)
    ids = jnp.broadcast_to(columns[0:1, 0:1], (8, LANES))
    code = ids & (SHARE - 1)
    late = jnp.where(lane8 == NEED + 1, (code >> 4) + 1, jnp.where(lane8 == NEED + 2, code & 15, 0))
    late = jnp.where(round_ref[0, 0] == 0, late, 0).astype(F32)
    for j in range(4):
        block = marks[j * BLOCK:(j + 1) * BLOCK]
        first = block[:LANES].T
        second = jnp.concatenate([block[LANES:], pltpu.roll(block[LANES:], 1, 1)], axis=0).T
        for q in range(4):
            special = jnp.where((ids >> 9) == 4 * q + j, late, 0.0)
            special = jnp.where(lane8 == NEED, need, special)
            tail = second[8 * q:8 * q + 8] + special
            meta_ref[4 * q + j] = jnp.where(
                row8 < 2, first[8 * q:8 * q + 8], jnp.where(row8 == 2, tail, 0.0)
            )


def route_kernel(
    spot_ref, place_ref, ids_ref, meta_ref, weight_hbm, got_ref,
    out_ref, firsts_ref, owned_ref, weight_ref, stage_ref, sems, got_sem, weight_sem,
):
    loaded = pltpu.make_async_copy(got_ref, owned_ref, got_sem)
    loaded.start()
    group = (spot_ref[0] * 4 + spot_ref[1]) * 2 + spot_ref[2]
    mine = pl.ds(pl.multiple_of(group * LANES, LANES), LANES)
    weight_load = pltpu.make_async_copy(weight_hbm.at[pl.ds(0, 256), mine], weight_ref, weight_sem)
    weight_load.start()
    columns = id_columns(ids_ref)
    rows = iota((4 * BLOCK, LANES), 0)
    selector = jnp.concatenate(
        [one_hot(rows == place_ref[:, c * LANES:(c + 1) * LANES]) for c in range(PARTS)], axis=1
    )
    weight_load.wait()
    loaded.wait()
    extras = [owned_ref[c, LANES:, :].astype(F32) for c in range(PARTS)]
    before = [jnp.zeros((16, LANES), F32)] + extras[:-1]
    firsts = finished_rows(
        [[extra[k:k + 1] for extra in before] for k in range(2)],
        [extra[2:3] + extra[3:4] + extra[4:5] for extra in extras],
        [extra[5:6, 0:1] for extra in extras],
        weight_ref[...],
    )
    firsts_ref[...] = firsts
    row16 = iota((16, LANES), 0)
    for c in range(1, PARTS):
        head = owned_ref[c, :16, :].astype(F32)
        owned_ref[c, :16, :] = jnp.where(row16 == 0, firsts[c:c + 1], head).astype(BF16)
    here = extras[0]
    late = stacked_rows(
        [0.0, 0.0, 0.0, extras[-1][0:1], extras[-1][1:2], here[2:3], here[3:4], here[4:5]], (8, LANES)
    )
    flag = (iota((8, LANES), 0) == 2) & (iota((8, LANES), 1) == NEED + 3)
    late = jnp.where(flag, here[5:6, 0:1], late)
    for half in range(2):
        wides = []
        for c in range(PARTS):
            quarter = columns[:, c:c + 1] >> 11
            latent = owned_ref[c, :LANES, :]
            wides.append(jnp.concatenate(
                [latent * one_hot(jnp.broadcast_to(quarter, (LANES, LANES)) == q) for q in (2 * half, 2 * half + 1)], axis=1
            ))
        total = jnp.dot(selector, jnp.concatenate(wides, axis=0), preferred_element_type=F32)
        for q in range(2):
            for j in range(4):
                to = 8 * half + 4 * q + j
                data = total[j * BLOCK:j * BLOCK + CAP, q * LANES:(q + 1) * LANES]
                stage_ref[to] = jnp.concatenate([data, meta_ref[to] + late], axis=0).astype(BF16)
                pltpu.make_async_copy(stage_ref.at[to], out_ref.at[to], sems.at[to]).start()
    for to in range(PARTS):
        pltpu.make_async_copy(stage_ref.at[to], out_ref.at[to], sems.at[to]).wait()


def update_kernel(
    spot_ref, message_ref, held_ref, ema_counts_ref, error_ref, picked_ref, weight_hbm, ema_sums_hbm,
    book_ref, counts_ref, kept_ref, error_out_ref, need_ref, ema_sums_ref, weight_ref, sems,
):
    group = (spot_ref[0] * 4 + spot_ref[1]) * 2 + spot_ref[2]
    mine = pl.ds(pl.multiple_of(group * LANES, LANES), LANES)
    weight_load = pltpu.make_async_copy(weight_hbm.at[pl.ds(0, 256), mine], weight_ref, sems.at[0])
    weight_load.start()
    sums_load = pltpu.make_async_copy(ema_sums_hbm, ema_sums_ref, sems.at[1])
    sums_load.start()
    codes = iota((SHARE, LANES), 0).astype(F32)
    ones = jnp.ones((8 * LANES, LANES), BF16)
    kept_ref[...] = held_ref[...]
    need = jnp.zeros((1, 1), F32)
    lane = iota((1, LANES), 1)
    metas, selectors, datas = [], [], []

    def flush():
        data = jnp.concatenate(datas, axis=0)
        kept_ref[...] += jnp.dot(
            jnp.concatenate(selectors, axis=1),
            jnp.concatenate([data, ones[:data.shape[0]]], axis=1),
            preferred_element_type=F32,
        )
        selectors.clear()
        datas.clear()

    for s in range(PARTS):
        meta = message_ref[s, BLOCK - 16:, :].astype(F32)[8:]
        metas.append(meta)
        need = jnp.maximum(need, meta[2:3, NEED:NEED + 1])
        selectors.append(one_hot(codes == (meta[0:1] - 1.0) * 16.0 + meta[1:2]))
        datas.append(message_ref[s, :LANES, :])
        if len(datas) == 8:
            flush()
    for s in range(0, PARTS, 2):
        tails = [meta[2:3] for meta in metas[s:s + 2]]
        turned = [pltpu.roll(jnp.broadcast_to(tail, (8, LANES)), 64, 1)[0:1] for tail in tails]
        high = jnp.where(lane < 64, tails[0], turned[1])
        low = jnp.where(lane < 64, turned[0], tails[1])
        high = jnp.where((lane & 63) < NEED, high, 0.0)
        selectors.append(one_hot(codes == (high - 1.0) * 16.0 + low))
        datas.append(
            jnp.concatenate([message_ref[s, LANES:, :], message_ref[s + 1, LANES:, :]], axis=0)
        )
        if len(datas) == 8:
            flush()

    weight_load.wait()
    before = [jnp.zeros((8, LANES), F32)] + metas[:-1]
    firsts = finished_rows(
        [[meta[k:k + 1] for meta in before] for k in (3, 4)],
        [meta[5:6] + meta[6:7] + meta[7:8] for meta in metas],
        [meta[2:3, NEED + 3:NEED + 4] for meta in metas],
        weight_ref[...],
    )
    wanted = jnp.full((1, LANES), -16.0, F32)
    for s in range(PARTS):
        high, low = metas[s][2:3, NEED + 1:NEED + 2], metas[s][2:3, NEED + 2:NEED + 3]
        wanted = jnp.where(lane == s, (high - 1.0) * 16.0 + low, wanted)
    selectors.append(one_hot(codes == wanted))
    datas.append(
        jnp.concatenate([firsts, jnp.zeros((LANES - PARTS, LANES), F32)], axis=0).astype(BF16)
    )
    flush()
    own = jnp.where(iota((PARTS, LANES), 0) == spot_ref[3], firsts, 0.0)
    diff = jnp.sum(own, axis=0, keepdims=True) - picked_ref[0:1]
    error = jnp.sum(diff * diff, axis=1, keepdims=True) * (1.0 / LANES)
    error_out_ref[...] = error_ref[...]
    error_out_ref[0:1, :LANES] = jnp.where(lane == 0, error, error_ref[0:1, :LANES])
    sums_load.wait()
    need_ref[0, 0] = jnp.max(need).astype(I32)
    diagonal = iota((LANES, LANES), 0) == iota((LANES, LANES), 1)
    for k in range(SHARE // LANES):
        begin = k * LANES
        old = jnp.broadcast_to(ema_counts_ref[0:1, begin:begin + LANES], (LANES, LANES)).T
        sums, counts = kept_ref[begin:begin + LANES, :LANES], kept_ref[begin:begin + LANES, LANES:]
        new_counts = ema_decay * old + (1.0 - ema_decay) * counts
        book_ref[begin:begin + LANES, :] = (
            ema_decay * ema_sums_ref[begin:begin + LANES, :] + (1.0 - ema_decay) * sums
        ) / new_counts
        counts_ref[0:1, begin:begin + LANES] = jnp.sum(
            jnp.where(diagonal, new_counts, 0.0), axis=0, keepdims=True
        )


def gather_kernel(near_ref, far_ref, beside_ref, across_ref, *out_refs):
    for k, ref in enumerate((near_ref, far_ref, beside_ref, across_ref)):
        for dy in range(1, 4):
            out_refs[dy - 1][k] = ref[dy]


def decode_kernel(
    place_ref, near_ref, far_ref, beside_ref, across_ref, y1_ref, y2_ref, y3_ref, weight_ref, out_ref
):
    groups = relative_blocks(place_ref)
    slabs, weights = [], []
    for dy in range(4):
        for k, ref in enumerate((near_ref, far_ref, beside_ref, across_ref)):
            group = groups[4 * k + (4 - dy) % 4]
            slabs.append(ref[0] if dy == 0 else (y1_ref, y2_ref, y3_ref)[dy - 1][k])
            weights.append(weight_ref[pl.ds(pl.multiple_of(group * LANES, LANES), LANES), :])
    decoded = jnp.dot(
        jnp.concatenate(slabs, axis=1), jnp.concatenate(weights, axis=0), preferred_element_type=F32
    ).astype(BF16)
    halves = jnp.concatenate([decoded[:, :256], decoded[:, 256:]], axis=0)
    row, col = iota((256, 256), 0), iota((256, 256), 1)
    source = (row >> 1) + (row & 1) * LANES
    out_ref[...] = jnp.dot(one_hot(col == source), halves, preferred_element_type=F32).astype(BF16)


def error_kernel(place_ref, firsts_ref, got_ref, near_ref, far_ref, beside_ref, error_ref, picked_ref):
    row = iota((LANES, LANES), 0)
    first = jnp.zeros((1, LANES), F32)
    for k, block in enumerate(relative_blocks(place_ref)):
        picked = (near_ref, far_ref)[k // 4][k % 4] if k < 8 else beside_ref[k - 8]
        picked = picked.astype(F32)
        first = jnp.where(block == 0, picked[0:1], first)
        latent = got_ref[block, :LANES, :].astype(F32)
        diff = jnp.where(row == 0, firsts_ref[pl.ds(block, 1), :], latent) - picked
        error = jnp.sum((diff * diff).T, axis=0, keepdims=True) * (1.0 / LANES)
        error_ref[0:1, pl.ds(pl.multiple_of(block * LANES, LANES), LANES)] = error
    picked_ref[...] = jnp.broadcast_to(first, (8, LANES))


def call(kernel, out_shape, count, flops, size, scalars=0, hbm_in=0, out_specs=None, scratch=(), aliases=None, limit=40):
    in_specs = [pl.BlockSpec(memory_space=pltpu.SMEM)] * scalars + [VMEM] * (count - scalars)
    in_specs[count - hbm_in:] = [IN_HBM] * hbm_in
    return pl.pallas_call(
        kernel,
        out_shape=out_shape,
        in_specs=in_specs,
        out_specs=out_specs or jax.tree.map(lambda _: VMEM, out_shape),
        scratch_shapes=list(scratch),
        input_output_aliases=aliases or {},
        cost_estimate=pl.CostEstimate(flops=flops, bytes_accessed=size, transcendentals=0),
        compiler_params=pltpu.CompilerParams(vmem_limit_bytes=limit << 20),
    )


def moved(shard, dx, dy, dc):
    pairs = [
        ((x * 4 + y) * 2 + c, ((x ^ dx) * 4 + (y + dy) % 4) * 2 + (c ^ dc))
        for x in range(2) for y in range(4) for c in range(2)
    ]
    return lax.ppermute(shard, "group", pairs)


def body(
    motion_frames, enc_weight, code_ids, clip_offsets, codebook, ema_sums, ema_counts, dec_weight
):
    shape = jax.ShapeDtypeStruct
    me = lax.axis_index("group").astype(I32)
    place = jnp.stack([me >> 3, (me >> 1) & 3, me & 1, lax.axis_index("dp").astype(I32)])
    blocks = shape((PARTS, TALL, LANES), BF16)
    four, eight = shape((4, LANES, LANES), BF16), shape((8, LANES, LANES), BF16)
    sent = call(
        encode_kernel, blocks, 3, 400 << 20, 4 << 20, hbm_in=3, limit=60, out_specs=IN_HBM,
        scratch=[
            pltpu.VMEM(motion_frames.shape, BF16),
            pltpu.VMEM(clip_offsets.shape, I32),
            pltpu.VMEM(enc_weight.shape, BF16),
            pltpu.VMEM(blocks.shape, BF16),
            pltpu.SemaphoreType.DMA((8,)),
            pltpu.SemaphoreType.DMA((PARTS,)),
        ],
    )(motion_frames, clip_offsets, enc_weight)
    sent, late_ids = lax.optimization_barrier((sent, code_ids))
    near, far, beside = call(pick_kernel, (four, four, eight), 3, 4 << 30, 4 << 20, scalars=1)(
        place, late_ids, codebook[0]
    )
    got = lax.all_to_all(sent, "group", split_axis=0, concat_axis=0)
    from_x = moved(beside, 1, 0, 0)
    from_core = moved(far, 0, 0, 1)

    def route(index):
        frame_places, meta = call(
            select_kernel,
            (shape((1, PARTS * LANES), I32), shape((PARTS, 8, LANES), F32)),
            2, 500 << 20, 1 << 20, scalars=1,
        )(index.reshape(1, 1), code_ids)
        message = shape((PARTS, BLOCK, LANES), BF16)
        return call(
            route_kernel, (message, shape((PARTS, LANES), F32)), 6, 2 << 30, 2 << 20, scalars=1, hbm_in=2,
            out_specs=(IN_HBM, VMEM), limit=60,
            scratch=[
                pltpu.VMEM(blocks.shape, BF16),
                pltpu.VMEM((256, LANES), BF16),
                pltpu.VMEM(message.shape, BF16),
                pltpu.SemaphoreType.DMA((PARTS,)),
                pltpu.SemaphoreType.DMA,
                pltpu.SemaphoreType.DMA,
            ],
        )(place, frame_places, code_ids, meta, enc_weight, got)

    def one_round(message, held):
        arrived = lax.all_to_all(message, "dp", split_axis=0, concat_axis=0)
        return call(
            update_kernel,
            (
                shape((SHARE, LANES), F32),
                shape((1, SHARE), F32),
                shape((SHARE, 2 * LANES), F32),
                shape((1, PARTS * LANES), F32),
                shape((1, 1), I32),
            ),
            8, 800 << 20, 2 << 20, scalars=1, hbm_in=2,
            out_specs=(VMEM, VMEM, VMEM, VMEM, pl.BlockSpec(memory_space=pltpu.SMEM)),
            scratch=[
                pltpu.VMEM((SHARE, LANES), F32),
                pltpu.VMEM((256, LANES), BF16),
                pltpu.SemaphoreType.DMA((2,)),
            ],
        )(place, arrived, held, ema_counts, error, first_picked, enc_weight, ema_sums[0])

    message, firsts = route(jnp.zeros((), I32))
    error, first_picked = call(
        error_kernel, (shape((1, PARTS * LANES), F32), shape((8, LANES), F32)), 6, 1 << 20, 1 << 20, scalars=1
    )(place, firsts, got, near, far, beside)
    message, from_x, from_core = lax.optimization_barrier((message, from_x, from_core))
    across = moved(from_x[4:], 0, 0, 1)
    columns = call(gather_kernel, (four,) * 3, 4, 1 << 20, 1 << 20)(near, from_core, from_x, across)
    columns = [moved(columns[dy - 1], 0, dy, 0) for dy in range(1, 4)]
    decoded = call(decode_kernel, shape((256, 256), BF16), 9, 300 << 20, 4 << 20, scalars=1)(
        place, near, from_core, from_x, across, *columns, dec_weight
    )

    first = one_round(message, jnp.zeros((SHARE, 2 * LANES), F32))

    def more(state):
        return state[0] < state[5][0, 0]

    def again(state):
        index, held = state[0], state[3]
        return (index + 1, *one_round(route(index)[0], held))

    _, new_codebook, new_counts, _, commit_error, _ = lax.while_loop(
        more, again, (jnp.ones((), I32), *first)
    )
    return (decoded, commit_error, new_codebook[None], new_counts)


def solution(mesh):
    return jax.shard_map(
        body,
        mesh=mesh,
        in_specs=(
            P(("dp", "group"), None),
            P(),
            P("group", "dp"),
            P(("dp", "group"), None),
            P("group", None, None),
            P("group", "dp", None),
            P("group", "dp"),
            P(),
        ),
        out_specs=(
            P(("dp", "group"), None),
            P("group", "dp"),
            P("group", "dp", None),
            P("group", "dp"),
        ),
        check_vma=False,
    )
```

```python
import jax
import jax.numpy as jnp
from jax import lax
from jax.experimental import pallas as pl
from jax.experimental.pallas import tpu as pltpu
from jax.sharding import PartitionSpec as P

ema_decay = 0.9

F32 = jnp.float32
BF16 = jnp.bfloat16
I32 = jnp.int32

LANES = 128
PARTS = 16
BLOCK = 192
CAP = 184
SHARE = 512
NEED = 56
TALL = 144

VMEM = pl.BlockSpec(memory_space=pltpu.VMEM)
IN_HBM = pl.BlockSpec(memory_space=pltpu.HBM)


def one_hot(condition):
    return jnp.where(condition, 1.0, 0.0).astype(BF16)


def iota(shape, axis):
    return lax.broadcasted_iota(I32, shape, axis)


def id_columns(ids_ref):
    rows = [ids_ref[0:1, c * LANES:(c + 1) * LANES] for c in range(PARTS)]
    return jnp.concatenate(rows, axis=0).T


def relative_blocks(place_ref):
    x, y, core = place_ref[0], place_ref[1], place_ref[2]
    return [
        ((x ^ dx) * 4 + ((y + dy) & 3)) * 2 + (core ^ dc)
        for dx in range(2) for dc in range(2) for dy in range(4)
    ]


def pick_kernel(place_ref, ids_ref, book_ref, near_ref, far_ref, beside_ref):
    blocks = relative_blocks(place_ref)
    rows = [ids_ref[0:1, pl.ds(pl.multiple_of(b * LANES, LANES), LANES)] for b in blocks]
    columns = jnp.concatenate(rows, axis=0).T
    lanes = iota((LANES, 1024), 1)
    step = 4
    for first in range(0, PARTS, step):
        ids = jnp.concatenate(
            [columns[:, c:c + 1] for c in range(first, first + step)], axis=0
        )
        low, top = ids & 1023, ids >> 10
        selector = jnp.concatenate(
            [one_hot(low[k * LANES:(k + 1) * LANES] == lanes) for k in range(step)], axis=0
        )
        picked = jnp.zeros((step * LANES, LANES), F32)
        for pair in range(4):
            begin = pair * 2048
            tile = jnp.concatenate(
                [book_ref[begin:begin + 1024, :], book_ref[begin + 1024:begin + 2048, :]], axis=1
            )
            both = jnp.dot(selector, tile, preferred_element_type=F32)
            picked = jnp.where(top == 2 * pair, both[:, :LANES], picked)
            picked = jnp.where(top == 2 * pair + 1, both[:, LANES:], picked)
        picked = picked.astype(BF16)
        for k in range(step):
            out_ref = (near_ref, far_ref, beside_ref)[min(first // 4, 2)]
            out_ref[(first + k) % (4 if first < 8 else 8)] = picked[k * LANES:(k + 1) * LANES]


def split3(values):
    first = values.astype(BF16).astype(F32)
    second = (values - first).astype(BF16).astype(F32)
    return first, second, values - first - second


def stacked_rows(rows, shape):
    row, table = iota(shape, 0), jnp.zeros(shape, F32)
    for k, values in enumerate(rows):
        table = jnp.where(row == k, values, table)
    return table


def encode_kernel(
    frames_hbm, clips_hbm, weight_hbm, out_ref, frames_ref, clips_ref, weight_ref, part_ref, stage_ref, in_sems, sems
):
    loads = [
        pltpu.make_async_copy(frames_hbm, frames_ref, in_sems.at[6]),
        pltpu.make_async_copy(clips_hbm, clips_ref, in_sems.at[7]),
    ]
    for k in range(6):
        rows = pl.ds(k * LANES, LANES)
        loads.append(
            pltpu.make_async_copy(weight_hbm.at[rows, :], weight_ref.at[rows, :], in_sems.at[k])
        )
    for load in loads:
        load.start()
    loads[0].wait()
    loads[1].wait()
    frames = frames_ref[...]
    row, col = iota((LANES, 256), 0), iota((LANES, 256), 1)
    even = jnp.dot(one_hot(col == 2 * row), frames, preferred_element_type=F32)
    odd = jnp.dot(one_hot(col == 2 * row + 1), frames, preferred_element_type=F32)
    earlier = jnp.dot(one_hot(col == 2 * row - 1), frames, preferred_element_type=F32)
    hits = jnp.where(iota((LANES, 8), 0) == clips_ref[...], 1.0, 0.0)
    starts = jnp.max(hits, axis=1, keepdims=True)
    earlier = jnp.where(starts > 0.0, 0.0, earlier)
    stacked = jnp.concatenate([earlier, even, odd], axis=1).astype(BF16)
    last = odd[LANES - 1:]
    for load in loads[2:6]:
        load.wait()
    for pair in range(PARTS // 2):
        strip = pl.ds(pair * 256, 256)
        part_ref[:, strip] = jnp.dot(
            stacked[:, :512], weight_ref[:512, strip], preferred_element_type=F32
        )
    for load in loads[6:]:
        load.wait()
    for pair in range(PARTS // 2):
        strip = pl.ds(pair * 256, 256)
        wide = part_ref[:, strip] + jnp.dot(
            stacked[:, 512:], weight_ref[512:, strip], preferred_element_type=F32
        )
        for g, block in ((2 * pair, wide[:, :LANES]), (2 * pair + 1, wide[:, LANES:])):
            extra = [last[:, :LANES], last[:, LANES:], *split3(block[:1]), starts[:1]]
            stage_ref[g, :LANES, :] = block.astype(BF16)
            stage_ref[g, LANES:, :] = stacked_rows(extra, (16, LANES)).astype(BF16)
            pltpu.make_async_copy(stage_ref.at[g], out_ref.at[g], sems.at[g]).start()
    for g in range(PARTS):
        pltpu.make_async_copy(stage_ref.at[g], out_ref.at[g], sems.at[g]).wait()


def finished_rows(lasts, parts, flags, weight):
    halo = jnp.concatenate(
        [jnp.concatenate(half, axis=0) for half in lasts], axis=1
    ).astype(BF16)
    added = jnp.dot(halo, weight, preferred_element_type=F32)
    added = jnp.where(jnp.concatenate(flags, axis=0) > 0.0, 0.0, added)
    return (added + jnp.concatenate(parts, axis=0)).astype(BF16).astype(F32)


def select_kernel(round_ref, ids_ref, place_ref, meta_ref):
    passed = round_ref[0, 0] * CAP
    dest_rows, tables = [], []
    sub16 = iota((PARTS, LANES), 0)
    for c in range(PARTS):
        dest = ids_ref[0:1, c * LANES:(c + 1) * LANES] >> 9
        dest_rows.append(dest)
        table = jnp.where(sub16 == dest, 1.0, 0.0)
        if c == 0:
            table = jnp.where(iota((PARTS, LANES), 1) == 0, 0.0, table)
        tables.append(table)
    upper = one_hot(iota((LANES, LANES), 0) <= iota((LANES, LANES), 1))
    cumulative = jnp.dot(
        jnp.concatenate(tables, axis=0).astype(BF16), upper, preferred_element_type=F32
    )
    offset = jnp.zeros((PARTS, 1), F32)
    rows = iota((4 * BLOCK, LANES), 0)
    selectors = []
    for c in range(PARTS):
        inside = cumulative[c * PARTS:(c + 1) * PARTS]
        rank = jnp.sum(tables[c] * (inside + (offset - 1.0)), axis=0, keepdims=True)
        rank = rank.astype(I32) - passed
        kept = (rank >= 0) & (rank < CAP)
        if c == 0:
            kept = kept & (iota((1, LANES), 1) > 0)
        place = jnp.where(kept, (dest_rows[c] & 3) * BLOCK + rank, -1)
        place_ref[:, c * LANES:(c + 1) * LANES] = place
        selectors.append(one_hot(rows == place))
        offset = offset + inside[:, LANES - 1:]
    most = jnp.max(offset, axis=0, keepdims=True)
    need = jnp.ones((1, 1), F32)
    for k in range(1, 2048 // CAP + 1):
        need = need + jnp.where(most > float(k * CAP), 1.0, 0.0)

    columns = id_columns(ids_ref)
    lane = iota((LANES, LANES), 1)
    pieces = []
    for c in range(PARTS):
        ids = columns[:, c:c + 1]
        code = ids & (SHARE - 1)
        mark = jnp.where((lane & 1) == 1, code & 15, (code >> 4) + 1)
        pieces.append(jnp.where((lane >> 3) == (ids >> 11), mark, 0).astype(F32).astype(BF16))
    marks = jnp.dot(
        jnp.concatenate(selectors, axis=1), jnp.concatenate(pieces, axis=0), preferred_element_type=F32
    )
    lane8, row8 = iota((8, LANES), 1), iota((8, LANES), 0)
    ids = jnp.broadcast_to(columns[0:1, 0:1], (8, LANES))
    code = ids & (SHARE - 1)
    late = jnp.where(lane8 == NEED + 1, (code >> 4) + 1, jnp.where(lane8 == NEED + 2, code & 15, 0))
    late = jnp.where(round_ref[0, 0] == 0, late, 0).astype(F32)
    for j in range(4):
        block = marks[j * BLOCK:(j + 1) * BLOCK]
        first = block[:LANES].T
        second = jnp.concatenate([block[LANES:], pltpu.roll(block[LANES:], 1, 1)], axis=0).T
        for q in range(4):
            special = jnp.where((ids >> 9) == 4 * q + j, late, 0.0)
            special = jnp.where(lane8 == NEED, need, special)
            tail = second[8 * q:8 * q + 8] + special
            meta_ref[4 * q + j] = jnp.where(
                row8 < 2, first[8 * q:8 * q + 8], jnp.where(row8 == 2, tail, 0.0)
            )


def route_kernel(
    spot_ref, place_ref, ids_ref, meta_ref, weight_hbm, got_ref,
    out_ref, firsts_ref, owned_ref, extra_ref, weight_ref, in_sems,
):
    group = (spot_ref[0] * 4 + spot_ref[1]) * 2 + spot_ref[2]
    mine = pl.ds(pl.multiple_of(group * LANES, LANES), LANES)
    extra_load = pltpu.make_async_copy(got_ref.at[:, pl.ds(LANES, 16), :], extra_ref, in_sems.at[0])
    weight_load = pltpu.make_async_copy(weight_hbm.at[pl.ds(0, 256), mine], weight_ref, in_sems.at[1])
    loaded = pltpu.make_async_copy(got_ref.at[:, pl.ds(0, LANES), :], owned_ref, in_sems.at[2])
    for load in (extra_load, weight_load, loaded):
        load.start()
    columns = id_columns(ids_ref)
    rows = iota((4 * BLOCK, LANES), 0)
    selector = jnp.concatenate(
        [one_hot(rows == place_ref[:, c * LANES:(c + 1) * LANES]) for c in range(PARTS)], axis=1
    )
    extra_load.wait()
    weight_load.wait()
    extras = [extra_ref[c].astype(F32) for c in range(PARTS)]
    before = [jnp.zeros((16, LANES), F32)] + extras[:-1]
    firsts = finished_rows(
        [[extra[k:k + 1] for extra in before] for k in range(2)],
        [extra[2:3] + extra[3:4] + extra[4:5] for extra in extras],
        [extra[5:6, 0:1] for extra in extras],
        weight_ref[...],
    )
    loaded.wait()
    firsts_ref[...] = firsts
    row16 = iota((16, LANES), 0)
    for c in range(1, PARTS):
        head = owned_ref[c, :16, :].astype(F32)
        owned_ref[c, :16, :] = jnp.where(row16 == 0, firsts[c:c + 1], head).astype(BF16)
    here = extras[0]
    late = stacked_rows(
        [0.0, 0.0, 0.0, extras[-1][0:1], extras[-1][1:2], here[2:3], here[3:4], here[4:5]], (8, LANES)
    )
    flag = (iota((8, LANES), 0) == 2) & (iota((8, LANES), 1) == NEED + 3)
    late = jnp.where(flag, here[5:6, 0:1], late)
    for half in range(2):
        wides = []
        for c in range(PARTS):
            quarter = columns[:, c:c + 1] >> 11
            latent = owned_ref[c]
            wides.append(jnp.concatenate(
                [latent * one_hot(jnp.broadcast_to(quarter, (LANES, LANES)) == q) for q in (2 * half, 2 * half + 1)], axis=1
            ))
        total = jnp.dot(selector, jnp.concatenate(wides, axis=0), preferred_element_type=F32)
        for q in range(2):
            for j in range(4):
                to = 8 * half + 4 * q + j
                data = total[j * BLOCK:j * BLOCK + CAP, q * LANES:(q + 1) * LANES]
                out_ref[to] = jnp.concatenate([data, meta_ref[to] + late], axis=0).astype(BF16)


def update_kernel(
    spot_ref, message_ref, held_ref, ema_counts_ref, error_ref, picked_ref, weight_hbm, ema_sums_hbm,
    book_ref, counts_ref, kept_ref, error_out_ref, need_ref, ema_sums_ref, weight_ref, sems,
):
    group = (spot_ref[0] * 4 + spot_ref[1]) * 2 + spot_ref[2]
    mine = pl.ds(pl.multiple_of(group * LANES, LANES), LANES)
    weight_load = pltpu.make_async_copy(weight_hbm.at[pl.ds(0, 256), mine], weight_ref, sems.at[0])
    weight_load.start()
    sums_load = pltpu.make_async_copy(ema_sums_hbm, ema_sums_ref, sems.at[1])
    sums_load.start()
    codes = iota((SHARE, LANES), 0).astype(F32)
    ones = jnp.ones((8 * LANES, LANES), BF16)
    kept_ref[...] = held_ref[...]
    need = jnp.zeros((1, 1), F32)
    lane = iota((1, LANES), 1)
    metas, selectors, datas = [], [], []

    def flush():
        data = jnp.concatenate(datas, axis=0)
        kept_ref[...] += jnp.dot(
            jnp.concatenate(selectors, axis=1),
            jnp.concatenate([data, ones[:data.shape[0]]], axis=1),
            preferred_element_type=F32,
        )
        selectors.clear()
        datas.clear()

    for s in range(PARTS):
        meta = message_ref[s, BLOCK - 16:, :].astype(F32)[8:]
        metas.append(meta)
        need = jnp.maximum(need, meta[2:3, NEED:NEED + 1])
        selectors.append(one_hot(codes == (meta[0:1] - 1.0) * 16.0 + meta[1:2]))
        datas.append(message_ref[s, :LANES, :])
        if len(datas) == 8:
            flush()
    for s in range(0, PARTS, 2):
        tails = [meta[2:3] for meta in metas[s:s + 2]]
        turned = [pltpu.roll(jnp.broadcast_to(tail, (8, LANES)), 64, 1)[0:1] for tail in tails]
        high = jnp.where(lane < 64, tails[0], turned[1])
        low = jnp.where(lane < 64, turned[0], tails[1])
        high = jnp.where((lane & 63) < NEED, high, 0.0)
        selectors.append(one_hot(codes == (high - 1.0) * 16.0 + low))
        datas.append(
            jnp.concatenate([message_ref[s, LANES:, :], message_ref[s + 1, LANES:, :]], axis=0)
        )
        if len(datas) == 8:
            flush()

    weight_load.wait()
    before = [jnp.zeros((8, LANES), F32)] + metas[:-1]
    firsts = finished_rows(
        [[meta[k:k + 1] for meta in before] for k in (3, 4)],
        [meta[5:6] + meta[6:7] + meta[7:8] for meta in metas],
        [meta[2:3, NEED + 3:NEED + 4] for meta in metas],
        weight_ref[...],
    )
    wanted = jnp.full((1, LANES), -16.0, F32)
    for s in range(PARTS):
        high, low = metas[s][2:3, NEED + 1:NEED + 2], metas[s][2:3, NEED + 2:NEED + 3]
        wanted = jnp.where(lane == s, (high - 1.0) * 16.0 + low, wanted)
    selectors.append(one_hot(codes == wanted))
    datas.append(
        jnp.concatenate([firsts, jnp.zeros((LANES - PARTS, LANES), F32)], axis=0).astype(BF16)
    )
    flush()
    own = jnp.where(iota((PARTS, LANES), 0) == spot_ref[3], firsts, 0.0)
    diff = jnp.sum(own, axis=0, keepdims=True) - picked_ref[0:1]
    error = jnp.sum(diff * diff, axis=1, keepdims=True) * (1.0 / LANES)
    error_out_ref[...] = error_ref[...]
    error_out_ref[0:1, :LANES] = jnp.where(lane == 0, error, error_ref[0:1, :LANES])
    sums_load.wait()
    need_ref[0, 0] = jnp.max(need).astype(I32)
    diagonal = iota((LANES, LANES), 0) == iota((LANES, LANES), 1)
    for k in range(SHARE // LANES):
        begin = k * LANES
        old = jnp.broadcast_to(ema_counts_ref[0:1, begin:begin + LANES], (LANES, LANES)).T
        sums, counts = kept_ref[begin:begin + LANES, :LANES], kept_ref[begin:begin + LANES, LANES:]
        new_counts = ema_decay * old + (1.0 - ema_decay) * counts
        book_ref[begin:begin + LANES, :] = (
            ema_decay * ema_sums_ref[begin:begin + LANES, :] + (1.0 - ema_decay) * sums
        ) / new_counts
        counts_ref[0:1, begin:begin + LANES] = jnp.sum(
            jnp.where(diagonal, new_counts, 0.0), axis=0, keepdims=True
        )


def gather_kernel(near_ref, far_ref, beside_ref, across_ref, *out_refs):
    for k, ref in enumerate((near_ref, far_ref, beside_ref, across_ref)):
        for dy in range(1, 4):
            out_refs[dy - 1][k] = ref[dy]


def decode_kernel(
    place_ref, near_ref, far_ref, beside_ref, across_ref, y1_ref, y2_ref, y3_ref, weight_ref, out_ref
):
    groups = relative_blocks(place_ref)
    slabs, weights = [], []
    for dy in range(4):
        for k, ref in enumerate((near_ref, far_ref, beside_ref, across_ref)):
            group = groups[4 * k + (4 - dy) % 4]
            slabs.append(ref[0] if dy == 0 else (y1_ref, y2_ref, y3_ref)[dy - 1][k])
            weights.append(weight_ref[pl.ds(pl.multiple_of(group * LANES, LANES), LANES), :])
    decoded = jnp.dot(
        jnp.concatenate(slabs, axis=1), jnp.concatenate(weights, axis=0), preferred_element_type=F32
    ).astype(BF16)
    halves = jnp.concatenate([decoded[:, :256], decoded[:, 256:]], axis=0)
    row, col = iota((256, 256), 0), iota((256, 256), 1)
    source = (row >> 1) + (row & 1) * LANES
    out_ref[...] = jnp.dot(one_hot(col == source), halves, preferred_element_type=F32).astype(BF16)


def error_kernel(place_ref, firsts_ref, got_ref, near_ref, far_ref, beside_ref, error_ref, picked_ref):
    row = iota((LANES, LANES), 0)
    first = jnp.zeros((1, LANES), F32)
    for k, block in enumerate(relative_blocks(place_ref)):
        picked = (near_ref, far_ref)[k // 4][k % 4] if k < 8 else beside_ref[k - 8]
        picked = picked.astype(F32)
        first = jnp.where(block == 0, picked[0:1], first)
        latent = got_ref[block, :LANES, :].astype(F32)
        diff = jnp.where(row == 0, firsts_ref[pl.ds(block, 1), :], latent) - picked
        error = jnp.sum((diff * diff).T, axis=0, keepdims=True) * (1.0 / LANES)
        error_ref[0:1, pl.ds(pl.multiple_of(block * LANES, LANES), LANES)] = error
    picked_ref[...] = jnp.broadcast_to(first, (8, LANES))


def call(kernel, out_shape, count, flops, size, scalars=0, hbm_in=0, out_specs=None, scratch=(), aliases=None, limit=40):
    in_specs = [pl.BlockSpec(memory_space=pltpu.SMEM)] * scalars + [VMEM] * (count - scalars)
    in_specs[count - hbm_in:] = [IN_HBM] * hbm_in
    return pl.pallas_call(
        kernel,
        out_shape=out_shape,
        in_specs=in_specs,
        out_specs=out_specs or jax.tree.map(lambda _: VMEM, out_shape),
        scratch_shapes=list(scratch),
        input_output_aliases=aliases or {},
        cost_estimate=pl.CostEstimate(flops=flops, bytes_accessed=size, transcendentals=0),
        compiler_params=pltpu.CompilerParams(vmem_limit_bytes=limit << 20),
    )


def moved(shard, dx, dy, dc):
    pairs = [
        ((x * 4 + y) * 2 + c, ((x ^ dx) * 4 + (y + dy) % 4) * 2 + (c ^ dc))
        for x in range(2) for y in range(4) for c in range(2)
    ]
    return lax.ppermute(shard, "group", pairs)


def body(
    motion_frames, enc_weight, code_ids, clip_offsets, codebook, ema_sums, ema_counts, dec_weight
):
    shape = jax.ShapeDtypeStruct
    me = lax.axis_index("group").astype(I32)
    place = jnp.stack([me >> 3, (me >> 1) & 3, me & 1, lax.axis_index("dp").astype(I32)])
    blocks = shape((PARTS, TALL, LANES), BF16)
    four, eight = shape((4, LANES, LANES), BF16), shape((8, LANES, LANES), BF16)
    sent = call(
        encode_kernel, blocks, 3, 400 << 20, 4 << 20, hbm_in=3, limit=60, out_specs=IN_HBM,
        scratch=[
            pltpu.VMEM(motion_frames.shape, BF16),
            pltpu.VMEM(clip_offsets.shape, I32),
            pltpu.VMEM(enc_weight.shape, BF16),
            pltpu.VMEM((LANES, enc_weight.shape[1]), F32),
            pltpu.VMEM(blocks.shape, BF16),
            pltpu.SemaphoreType.DMA((8,)),
            pltpu.SemaphoreType.DMA((PARTS,)),
        ],
    )(motion_frames, clip_offsets, enc_weight)
    sent, late_ids = lax.optimization_barrier((sent, code_ids))
    near, far, beside = call(pick_kernel, (four, four, eight), 3, 4 << 30, 4 << 20, scalars=1)(
        place, late_ids, codebook[0]
    )
    got = lax.all_to_all(sent, "group", split_axis=0, concat_axis=0)
    from_x = moved(beside, 1, 0, 0)
    from_core = moved(far, 0, 0, 1)

    def route(index):
        frame_places, meta = call(
            select_kernel,
            (shape((1, PARTS * LANES), I32), shape((PARTS, 8, LANES), F32)),
            2, 500 << 20, 1 << 20, scalars=1,
        )(index.reshape(1, 1), code_ids)
        message = shape((PARTS, BLOCK, LANES), BF16)
        return call(
            route_kernel, (message, shape((PARTS, LANES), F32)), 6, 2 << 30, 2 << 20, scalars=1, hbm_in=2,
            scratch=[
                pltpu.VMEM((PARTS, LANES, LANES), BF16),
                pltpu.VMEM((PARTS, 16, LANES), BF16),
                pltpu.VMEM((256, LANES), BF16),
                pltpu.SemaphoreType.DMA((3,)),
            ],
        )(place, frame_places, code_ids, meta, enc_weight, got)

    def one_round(message, held):
        arrived = lax.all_to_all(message, "dp", split_axis=0, concat_axis=0)
        return call(
            update_kernel,
            (
                shape((SHARE, LANES), F32),
                shape((1, SHARE), F32),
                shape((SHARE, 2 * LANES), F32),
                shape((1, PARTS * LANES), F32),
                shape((1, 1), I32),
            ),
            8, 800 << 20, 2 << 20, scalars=1, hbm_in=2,
            out_specs=(VMEM, VMEM, VMEM, VMEM, pl.BlockSpec(memory_space=pltpu.SMEM)),
            scratch=[
                pltpu.VMEM((SHARE, LANES), F32),
                pltpu.VMEM((256, LANES), BF16),
                pltpu.SemaphoreType.DMA((2,)),
            ],
        )(place, arrived, held, ema_counts, error, first_picked, enc_weight, ema_sums[0])

    message, firsts = route(jnp.zeros((), I32))
    error, first_picked = call(
        error_kernel, (shape((1, PARTS * LANES), F32), shape((8, LANES), F32)), 6, 1 << 20, 1 << 20, scalars=1
    )(place, firsts, got, near, far, beside)
    message, from_x, from_core = lax.optimization_barrier((message, from_x, from_core))
    across = moved(from_x[4:], 0, 0, 1)
    columns = call(gather_kernel, (four,) * 3, 4, 1 << 20, 1 << 20)(near, from_core, from_x, across)
    columns = [moved(columns[dy - 1], 0, dy, 0) for dy in range(1, 4)]
    decoded = call(decode_kernel, shape((256, 256), BF16), 9, 300 << 20, 4 << 20, scalars=1)(
        place, near, from_core, from_x, across, *columns, dec_weight
    )

    first = one_round(message, jnp.zeros((SHARE, 2 * LANES), F32))

    def more(state):
        return state[0] < state[5][0, 0]

    def again(state):
        index, held = state[0], state[3]
        return (index + 1, *one_round(route(index)[0], held))

    _, new_codebook, new_counts, _, commit_error, _ = lax.while_loop(
        more, again, (jnp.ones((), I32), *first)
    )
    return (decoded, commit_error, new_codebook[None], new_counts)


def solution(mesh):
    return jax.shard_map(
        body,
        mesh=mesh,
        in_specs=(
            P(("dp", "group"), None),
            P(),
            P("group", "dp"),
            P(("dp", "group"), None),
            P("group", None, None),
            P("group", "dp", None),
            P("group", "dp"),
            P(),
        ),
        out_specs=(
            P(("dp", "group"), None),
            P("group", "dp"),
            P("group", "dp", None),
            P("group", "dp"),
        ),
        check_vma=False,
    )
```

```python
import functools

import jax
import jax.numpy as jnp
from jax import lax
from jax.experimental import pallas as pl
from jax.experimental.pallas import tpu as pltpu
from jax.sharding import PartitionSpec as P

ema_decay = 0.9

F32 = jnp.float32
BF16 = jnp.bfloat16
I32 = jnp.int32

LANES = 128
PARTS = 16
BLOCK = 192
CAP = 184
SHARE = 512
NEED = 56
TALL = 144

VMEM = pl.BlockSpec(memory_space=pltpu.VMEM)
IN_HBM = pl.BlockSpec(memory_space=pltpu.HBM)


def one_hot(condition):
    return jnp.where(condition, 1.0, 0.0).astype(BF16)


def iota(shape, axis):
    return lax.broadcasted_iota(I32, shape, axis)


def id_columns(ids_ref):
    rows = [ids_ref[0:1, c * LANES:(c + 1) * LANES] for c in range(PARTS)]
    return jnp.concatenate(rows, axis=0).T


def relative_blocks(place_ref):
    x, y, core = place_ref[0], place_ref[1], place_ref[2]
    return [
        ((x ^ dx) * 4 + ((y + dy) & 3)) * 2 + (core ^ dc)
        for dx in range(2) for dc in range(2) for dy in range(4)
    ]


def pick_kernel(place_ref, ids_ref, book_ref, near_ref, far_ref, beside_ref):
    blocks = relative_blocks(place_ref)
    rows = [ids_ref[0:1, pl.ds(pl.multiple_of(b * LANES, LANES), LANES)] for b in blocks]
    columns = jnp.concatenate(rows, axis=0).T
    lanes = iota((LANES, 1024), 1)
    step = 4
    for first in range(0, PARTS, step):
        ids = jnp.concatenate(
            [columns[:, c:c + 1] for c in range(first, first + step)], axis=0
        )
        low, top = ids & 1023, ids >> 10
        selector = jnp.concatenate(
            [one_hot(low[k * LANES:(k + 1) * LANES] == lanes) for k in range(step)], axis=0
        )
        picked = jnp.zeros((step * LANES, LANES), F32)
        for pair in range(4):
            begin = pair * 2048
            tile = jnp.concatenate(
                [book_ref[begin:begin + 1024, :], book_ref[begin + 1024:begin + 2048, :]], axis=1
            )
            both = jnp.dot(selector, tile, preferred_element_type=F32)
            picked = jnp.where(top == 2 * pair, both[:, :LANES], picked)
            picked = jnp.where(top == 2 * pair + 1, both[:, LANES:], picked)
        picked = picked.astype(BF16)
        for k in range(step):
            out_ref = (near_ref, far_ref, beside_ref)[min(first // 4, 2)]
            out_ref[(first + k) % (4 if first < 8 else 8)] = picked[k * LANES:(k + 1) * LANES]


def split3(values):
    first = values.astype(BF16).astype(F32)
    second = (values - first).astype(BF16).astype(F32)
    return first, second, values - first - second


def stacked_rows(rows, shape):
    row, table = iota(shape, 0), jnp.zeros(shape, F32)
    for k, values in enumerate(rows):
        table = jnp.where(row == k, values, table)
    return table


def encode_kernel(
    frames_hbm, clips_hbm, weight_hbm, out_ref, frames_ref, clips_ref, weight_ref, part_ref, stage_ref, in_sems, sems
):
    loads = [
        pltpu.make_async_copy(frames_hbm, frames_ref, in_sems.at[6]),
        pltpu.make_async_copy(clips_hbm, clips_ref, in_sems.at[7]),
    ]
    for k in range(6):
        rows = pl.ds(k * LANES, LANES)
        loads.append(
            pltpu.make_async_copy(weight_hbm.at[rows, :], weight_ref.at[rows, :], in_sems.at[k])
        )
    for load in loads:
        load.start()
    loads[0].wait()
    loads[1].wait()
    frames = frames_ref[...]
    row, col = iota((LANES, 256), 0), iota((LANES, 256), 1)
    even = jnp.dot(one_hot(col == 2 * row), frames, preferred_element_type=F32)
    odd = jnp.dot(one_hot(col == 2 * row + 1), frames, preferred_element_type=F32)
    earlier = jnp.dot(one_hot(col == 2 * row - 1), frames, preferred_element_type=F32)
    hits = jnp.where(iota((LANES, 8), 0) == clips_ref[...], 1.0, 0.0)
    starts = jnp.max(hits, axis=1, keepdims=True)
    earlier = jnp.where(starts > 0.0, 0.0, earlier)
    stacked = jnp.concatenate([earlier, even, odd], axis=1).astype(BF16)
    last = odd[LANES - 1:]
    for load in loads[2:6]:
        load.wait()
    for pair in range(PARTS // 2):
        strip = pl.ds(pair * 256, 256)
        part_ref[:, strip] = jnp.dot(
            stacked[:, :512], weight_ref[:512, strip], preferred_element_type=F32
        )
    for load in loads[6:]:
        load.wait()
    for pair in range(PARTS // 2):
        strip = pl.ds(pair * 256, 256)
        wide = part_ref[:, strip] + jnp.dot(
            stacked[:, 512:], weight_ref[512:, strip], preferred_element_type=F32
        )
        for g, block in ((2 * pair, wide[:, :LANES]), (2 * pair + 1, wide[:, LANES:])):
            extra = [last[:, :LANES], last[:, LANES:], *split3(block[:1]), starts[:1]]
            stage_ref[g, :LANES, :] = block.astype(BF16)
            stage_ref[g, LANES:, :] = stacked_rows(extra, (16, LANES)).astype(BF16)
            pltpu.make_async_copy(stage_ref.at[g], out_ref.at[g], sems.at[g]).start()
    for g in range(PARTS):
        pltpu.make_async_copy(stage_ref.at[g], out_ref.at[g], sems.at[g]).wait()


def finished_rows(lasts, parts, flags, weight):
    halo = jnp.concatenate(
        [jnp.concatenate(half, axis=0) for half in lasts], axis=1
    ).astype(BF16)
    added = jnp.dot(halo, weight, preferred_element_type=F32)
    added = jnp.where(jnp.concatenate(flags, axis=0) > 0.0, 0.0, added)
    return (added + jnp.concatenate(parts, axis=0)).astype(BF16).astype(F32)


def select_kernel(round_ref, ids_ref, place_ref, meta_ref):
    passed = round_ref[0, 0] * CAP
    dest_rows, tables = [], []
    sub16 = iota((PARTS, LANES), 0)
    for c in range(PARTS):
        dest = ids_ref[0:1, c * LANES:(c + 1) * LANES] >> 9
        dest_rows.append(dest)
        table = jnp.where(sub16 == dest, 1.0, 0.0)
        if c == 0:
            table = jnp.where(iota((PARTS, LANES), 1) == 0, 0.0, table)
        tables.append(table)
    upper = one_hot(iota((LANES, LANES), 0) <= iota((LANES, LANES), 1))
    cumulative = jnp.dot(
        jnp.concatenate(tables, axis=0).astype(BF16), upper, preferred_element_type=F32
    )
    offset = jnp.zeros((PARTS, 1), F32)
    rows = iota((4 * BLOCK, LANES), 0)
    selectors = []
    for c in range(PARTS):
        inside = cumulative[c * PARTS:(c + 1) * PARTS]
        rank = jnp.sum(tables[c] * (inside + (offset - 1.0)), axis=0, keepdims=True)
        rank = rank.astype(I32) - passed
        kept = (rank >= 0) & (rank < CAP)
        if c == 0:
            kept = kept & (iota((1, LANES), 1) > 0)
        place = jnp.where(kept, (dest_rows[c] & 3) * BLOCK + rank, -1)
        place_ref[:, c * LANES:(c + 1) * LANES] = place
        selectors.append(one_hot(rows == place))
        offset = offset + inside[:, LANES - 1:]
    most = jnp.max(offset, axis=0, keepdims=True)
    need = jnp.ones((1, 1), F32)
    for k in range(1, 2048 // CAP + 1):
        need = need + jnp.where(most > float(k * CAP), 1.0, 0.0)

    columns = id_columns(ids_ref)
    lane = iota((LANES, LANES), 1)
    pieces = []
    for c in range(PARTS):
        ids = columns[:, c:c + 1]
        code = ids & (SHARE - 1)
        mark = jnp.where((lane & 1) == 1, code & 15, (code >> 4) + 1)
        pieces.append(jnp.where((lane >> 3) == (ids >> 11), mark, 0).astype(F32).astype(BF16))
    marks = jnp.dot(
        jnp.concatenate(selectors, axis=1), jnp.concatenate(pieces, axis=0), preferred_element_type=F32
    )
    lane8, row8 = iota((8, LANES), 1), iota((8, LANES), 0)
    ids = jnp.broadcast_to(columns[0:1, 0:1], (8, LANES))
    code = ids & (SHARE - 1)
    late = jnp.where(lane8 == NEED + 1, (code >> 4) + 1, jnp.where(lane8 == NEED + 2, code & 15, 0))
    late = jnp.where(round_ref[0, 0] == 0, late, 0).astype(F32)
    for j in range(4):
        block = marks[j * BLOCK:(j + 1) * BLOCK]
        first = block[:LANES].T
        second = jnp.concatenate([block[LANES:], pltpu.roll(block[LANES:], 1, 1)], axis=0).T
        for q in range(4):
            special = jnp.where((ids >> 9) == 4 * q + j, late, 0.0)
            special = jnp.where(lane8 == NEED, need, special)
            tail = second[8 * q:8 * q + 8] + special
            meta_ref[4 * q + j] = jnp.where(
                row8 < 2, first[8 * q:8 * q + 8], jnp.where(row8 == 2, tail, 0.0)
            )


def route_kernel(
    spot_ref, place_ref, ids_ref, meta_ref, weight_hbm, got_ref,
    out_ref, firsts_ref, owned_ref, extra_ref, weight_ref, in_sems,
):
    group = (spot_ref[0] * 4 + spot_ref[1]) * 2 + spot_ref[2]
    mine = pl.ds(pl.multiple_of(group * LANES, LANES), LANES)
    extra_load = pltpu.make_async_copy(got_ref.at[:, pl.ds(LANES, 16), :], extra_ref, in_sems.at[0])
    weight_load = pltpu.make_async_copy(weight_hbm.at[pl.ds(0, 256), mine], weight_ref, in_sems.at[1])
    loaded = pltpu.make_async_copy(got_ref.at[:, pl.ds(0, LANES), :], owned_ref, in_sems.at[2])
    for load in (extra_load, weight_load, loaded):
        load.start()
    columns = id_columns(ids_ref)
    rows = iota((4 * BLOCK, LANES), 0)
    selector = jnp.concatenate(
        [one_hot(rows == place_ref[:, c * LANES:(c + 1) * LANES]) for c in range(PARTS)], axis=1
    )
    extra_load.wait()
    weight_load.wait()
    extras = [extra_ref[c].astype(F32) for c in range(PARTS)]
    before = [jnp.zeros((16, LANES), F32)] + extras[:-1]
    firsts = finished_rows(
        [[extra[k:k + 1] for extra in before] for k in range(2)],
        [extra[2:3] + extra[3:4] + extra[4:5] for extra in extras],
        [extra[5:6, 0:1] for extra in extras],
        weight_ref[...],
    )
    loaded.wait()
    firsts_ref[...] = firsts
    row16 = iota((16, LANES), 0)
    for c in range(1, PARTS):
        head = owned_ref[c, :16, :].astype(F32)
        owned_ref[c, :16, :] = jnp.where(row16 == 0, firsts[c:c + 1], head).astype(BF16)
    here = extras[0]
    late = stacked_rows(
        [0.0, 0.0, 0.0, extras[-1][0:1], extras[-1][1:2], here[2:3], here[3:4], here[4:5]], (8, LANES)
    )
    flag = (iota((8, LANES), 0) == 2) & (iota((8, LANES), 1) == NEED + 3)
    late = jnp.where(flag, here[5:6, 0:1], late)
    for half in range(2):
        wides = []
        for c in range(PARTS):
            quarter = columns[:, c:c + 1] >> 11
            latent = owned_ref[c]
            wides.append(jnp.concatenate(
                [latent * one_hot(jnp.broadcast_to(quarter, (LANES, LANES)) == q) for q in (2 * half, 2 * half + 1)], axis=1
            ))
        total = jnp.dot(selector, jnp.concatenate(wides, axis=0), preferred_element_type=F32)
        for q in range(2):
            for j in range(4):
                to = 8 * half + 4 * q + j
                data = total[j * BLOCK:j * BLOCK + CAP, q * LANES:(q + 1) * LANES]
                out_ref[to] = jnp.concatenate([data, meta_ref[to] + late], axis=0).astype(BF16)


def update_kernel(
    fresh, spot_ref, message_ref, held_ref, ema_counts_ref, error_ref, picked_ref, weight_hbm, ema_sums_hbm,
    book_ref, counts_ref, kept_ref, error_out_ref, need_ref, ema_sums_ref, weight_ref, sems,
):
    group = (spot_ref[0] * 4 + spot_ref[1]) * 2 + spot_ref[2]
    mine = pl.ds(pl.multiple_of(group * LANES, LANES), LANES)
    weight_load = pltpu.make_async_copy(weight_hbm.at[pl.ds(0, 256), mine], weight_ref, sems.at[0])
    weight_load.start()
    sums_load = pltpu.make_async_copy(ema_sums_hbm, ema_sums_ref, sems.at[1])
    sums_load.start()
    codes = iota((SHARE, LANES), 0).astype(F32)
    ones = jnp.ones((8 * LANES, LANES), BF16)
    if not fresh:
        kept_ref[...] = held_ref[...]
    need = jnp.zeros((1, 1), F32)
    lane = iota((1, LANES), 1)
    metas, selectors, datas, begun = [], [], [], []

    def flush():
        data = jnp.concatenate(datas, axis=0)
        product = jnp.dot(
            jnp.concatenate(selectors, axis=1),
            jnp.concatenate([data, ones[:data.shape[0]]], axis=1),
            preferred_element_type=F32,
        )
        if fresh and not begun:
            kept_ref[...] = product
        else:
            kept_ref[...] += product
        begun.append(True)
        selectors.clear()
        datas.clear()

    for s in range(PARTS):
        meta = message_ref[s, BLOCK - 16:, :].astype(F32)[8:]
        metas.append(meta)
        need = jnp.maximum(need, meta[2:3, NEED:NEED + 1])
        selectors.append(one_hot(codes == (meta[0:1] - 1.0) * 16.0 + meta[1:2]))
        datas.append(message_ref[s, :LANES, :])
        if len(datas) == 8:
            flush()
    for s in range(0, PARTS, 2):
        tails = [meta[2:3] for meta in metas[s:s + 2]]
        turned = [pltpu.roll(jnp.broadcast_to(tail, (8, LANES)), 64, 1)[0:1] for tail in tails]
        high = jnp.where(lane < 64, tails[0], turned[1])
        low = jnp.where(lane < 64, turned[0], tails[1])
        high = jnp.where((lane & 63) < NEED, high, 0.0)
        selectors.append(one_hot(codes == (high - 1.0) * 16.0 + low))
        datas.append(
            jnp.concatenate([message_ref[s, LANES:, :], message_ref[s + 1, LANES:, :]], axis=0)
        )
        if len(datas) == 8:
            flush()

    weight_load.wait()
    before = [jnp.zeros((8, LANES), F32)] + metas[:-1]
    firsts = finished_rows(
        [[meta[k:k + 1] for meta in before] for k in (3, 4)],
        [meta[5:6] + meta[6:7] + meta[7:8] for meta in metas],
        [meta[2:3, NEED + 3:NEED + 4] for meta in metas],
        weight_ref[...],
    )
    wanted = jnp.full((1, LANES), -16.0, F32)
    for s in range(PARTS):
        high, low = metas[s][2:3, NEED + 1:NEED + 2], metas[s][2:3, NEED + 2:NEED + 3]
        wanted = jnp.where(lane == s, (high - 1.0) * 16.0 + low, wanted)
    selectors.append(one_hot(codes == wanted))
    datas.append(
        jnp.concatenate([firsts, jnp.zeros((LANES - PARTS, LANES), F32)], axis=0).astype(BF16)
    )
    flush()
    own = jnp.where(iota((PARTS, LANES), 0) == spot_ref[3], firsts, 0.0)
    diff = jnp.sum(own, axis=0, keepdims=True) - picked_ref[0:1]
    error = jnp.sum(diff * diff, axis=1, keepdims=True) * (1.0 / LANES)
    error_out_ref[...] = error_ref[...]
    error_out_ref[0:1, :LANES] = jnp.where(lane == 0, error, error_ref[0:1, :LANES])
    sums_load.wait()
    need_ref[0, 0] = jnp.max(need).astype(I32)
    diagonal = iota((LANES, LANES), 0) == iota((LANES, LANES), 1)
    for k in range(SHARE // LANES):
        begin = k * LANES
        old = jnp.broadcast_to(ema_counts_ref[0:1, begin:begin + LANES], (LANES, LANES)).T
        sums, counts = kept_ref[begin:begin + LANES, :LANES], kept_ref[begin:begin + LANES, LANES:]
        new_counts = ema_decay * old + (1.0 - ema_decay) * counts
        book_ref[begin:begin + LANES, :] = (
            ema_decay * ema_sums_ref[begin:begin + LANES, :] + (1.0 - ema_decay) * sums
        ) / new_counts
        counts_ref[0:1, begin:begin + LANES] = jnp.sum(
            jnp.where(diagonal, new_counts, 0.0), axis=0, keepdims=True
        )


def gather_kernel(near_ref, far_ref, beside_ref, across_ref, *out_refs):
    for k, ref in enumerate((near_ref, far_ref, beside_ref, across_ref)):
        for dy in range(1, 4):
            out_refs[dy - 1][k] = ref[dy]


def decode_kernel(
    place_ref, near_ref, far_ref, beside_ref, across_ref, y1_ref, y2_ref, y3_ref, weight_ref, out_ref
):
    groups = relative_blocks(place_ref)
    slabs, weights = [], []
    for dy in range(4):
        for k, ref in enumerate((near_ref, far_ref, beside_ref, across_ref)):
            group = groups[4 * k + (4 - dy) % 4]
            slabs.append(ref[0] if dy == 0 else (y1_ref, y2_ref, y3_ref)[dy - 1][k])
            weights.append(weight_ref[pl.ds(pl.multiple_of(group * LANES, LANES), LANES), :])
    decoded = jnp.dot(
        jnp.concatenate(slabs, axis=1), jnp.concatenate(weights, axis=0), preferred_element_type=F32
    ).astype(BF16)
    halves = jnp.concatenate([decoded[:, :256], decoded[:, 256:]], axis=0)
    row, col = iota((256, 256), 0), iota((256, 256), 1)
    source = (row >> 1) + (row & 1) * LANES
    out_ref[...] = jnp.dot(one_hot(col == source), halves, preferred_element_type=F32).astype(BF16)


def error_kernel(place_ref, firsts_ref, got_ref, near_ref, far_ref, beside_ref, error_ref, picked_ref):
    row = iota((LANES, LANES), 0)
    first = jnp.zeros((1, LANES), F32)
    for k, block in enumerate(relative_blocks(place_ref)):
        picked = (near_ref, far_ref)[k // 4][k % 4] if k < 8 else beside_ref[k - 8]
        picked = picked.astype(F32)
        first = jnp.where(block == 0, picked[0:1], first)
        latent = got_ref[block, :LANES, :].astype(F32)
        diff = jnp.where(row == 0, firsts_ref[pl.ds(block, 1), :], latent) - picked
        error = jnp.sum((diff * diff).T, axis=0, keepdims=True) * (1.0 / LANES)
        error_ref[0:1, pl.ds(pl.multiple_of(block * LANES, LANES), LANES)] = error
    picked_ref[...] = jnp.broadcast_to(first, (8, LANES))


def call(kernel, out_shape, count, flops, size, scalars=0, hbm_in=0, out_specs=None, scratch=(), aliases=None, limit=40):
    in_specs = [pl.BlockSpec(memory_space=pltpu.SMEM)] * scalars + [VMEM] * (count - scalars)
    in_specs[count - hbm_in:] = [IN_HBM] * hbm_in
    return pl.pallas_call(
        kernel,
        out_shape=out_shape,
        in_specs=in_specs,
        out_specs=out_specs or jax.tree.map(lambda _: VMEM, out_shape),
        scratch_shapes=list(scratch),
        input_output_aliases=aliases or {},
        cost_estimate=pl.CostEstimate(flops=flops, bytes_accessed=size, transcendentals=0),
        compiler_params=pltpu.CompilerParams(vmem_limit_bytes=limit << 20),
    )


def moved(shard, dx, dy, dc):
    pairs = [
        ((x * 4 + y) * 2 + c, ((x ^ dx) * 4 + (y + dy) % 4) * 2 + (c ^ dc))
        for x in range(2) for y in range(4) for c in range(2)
    ]
    return lax.ppermute(shard, "group", pairs)


def body(
    motion_frames, enc_weight, code_ids, clip_offsets, codebook, ema_sums, ema_counts, dec_weight
):
    shape = jax.ShapeDtypeStruct
    me = lax.axis_index("group").astype(I32)
    place = jnp.stack([me >> 3, (me >> 1) & 3, me & 1, lax.axis_index("dp").astype(I32)])
    blocks = shape((PARTS, TALL, LANES), BF16)
    four, eight = shape((4, LANES, LANES), BF16), shape((8, LANES, LANES), BF16)
    sent = call(
        encode_kernel, blocks, 3, 400 << 20, 4 << 20, hbm_in=3, limit=60, out_specs=IN_HBM,
        scratch=[
            pltpu.VMEM(motion_frames.shape, BF16),
            pltpu.VMEM(clip_offsets.shape, I32),
            pltpu.VMEM(enc_weight.shape, BF16),
            pltpu.VMEM((LANES, enc_weight.shape[1]), F32),
            pltpu.VMEM(blocks.shape, BF16),
            pltpu.SemaphoreType.DMA((8,)),
            pltpu.SemaphoreType.DMA((PARTS,)),
        ],
    )(motion_frames, clip_offsets, enc_weight)
    sent, late_ids = lax.optimization_barrier((sent, code_ids))
    near, far, beside = call(pick_kernel, (four, four, eight), 3, 4 << 30, 4 << 20, scalars=1)(
        place, late_ids, codebook[0]
    )
    got = lax.all_to_all(sent, "group", split_axis=0, concat_axis=0)
    from_x = moved(beside, 1, 0, 0)
    from_core = moved(far, 0, 0, 1)

    def route(index):
        frame_places, meta = call(
            select_kernel,
            (shape((1, PARTS * LANES), I32), shape((PARTS, 8, LANES), F32)),
            2, 500 << 20, 1 << 20, scalars=1,
        )(index.reshape(1, 1), code_ids)
        message = shape((PARTS, BLOCK, LANES), BF16)
        return call(
            route_kernel, (message, shape((PARTS, LANES), F32)), 6, 2 << 30, 2 << 20, scalars=1, hbm_in=2,
            scratch=[
                pltpu.VMEM((PARTS, LANES, LANES), BF16),
                pltpu.VMEM((PARTS, 16, LANES), BF16),
                pltpu.VMEM((256, LANES), BF16),
                pltpu.SemaphoreType.DMA((3,)),
            ],
        )(place, frame_places, code_ids, meta, enc_weight, got)

    def one_round(message, held, fresh=False):
        arrived = lax.all_to_all(message, "dp", split_axis=0, concat_axis=0)
        return call(
            functools.partial(update_kernel, fresh),
            (
                shape((SHARE, LANES), F32),
                shape((1, SHARE), F32),
                shape((SHARE, 2 * LANES), F32),
                shape((1, PARTS * LANES), F32),
                shape((1, 1), I32),
            ),
            8, 800 << 20, 2 << 20, scalars=1, hbm_in=2,
            out_specs=(VMEM, VMEM, VMEM, VMEM, pl.BlockSpec(memory_space=pltpu.SMEM)),
            scratch=[
                pltpu.VMEM((SHARE, LANES), F32),
                pltpu.VMEM((256, LANES), BF16),
                pltpu.SemaphoreType.DMA((2,)),
            ],
        )(place, arrived, held, ema_counts, error, first_picked, enc_weight, ema_sums[0])

    message, firsts = route(jnp.zeros((), I32))
    error, first_picked = call(
        error_kernel, (shape((1, PARTS * LANES), F32), shape((8, LANES), F32)), 6, 1 << 20, 1 << 20, scalars=1
    )(place, firsts, got, near, far, beside)
    message, from_x, from_core = lax.optimization_barrier((message, from_x, from_core))
    across = moved(from_x[4:], 0, 0, 1)
    columns = call(gather_kernel, (four,) * 3, 4, 1 << 20, 1 << 20)(near, from_core, from_x, across)
    columns = [moved(columns[dy - 1], 0, dy, 0) for dy in range(1, 4)]
    decoded = call(decode_kernel, shape((256, 256), BF16), 9, 300 << 20, 4 << 20, scalars=1)(
        place, near, from_core, from_x, across, *columns, dec_weight
    )

    first = one_round(message, jnp.zeros((SHARE, 2 * LANES), F32), True)

    def more(state):
        return state[0] < state[5][0, 0]

    def again(state):
        index, held = state[0], state[3]
        return (index + 1, *one_round(route(index)[0], held))

    _, new_codebook, new_counts, _, commit_error, _ = lax.while_loop(
        more, again, (jnp.ones((), I32), *first)
    )
    return (decoded, commit_error, new_codebook[None], new_counts)


def solution(mesh):
    return jax.shard_map(
        body,
        mesh=mesh,
        in_specs=(
            P(("dp", "group"), None),
            P(),
            P("group", "dp"),
            P(("dp", "group"), None),
            P("group", None, None),
            P("group", "dp", None),
            P("group", "dp"),
            P(),
        ),
        out_specs=(
            P(("dp", "group"), None),
            P("group", "dp"),
            P("group", "dp", None),
            P("group", "dp"),
        ),
        check_vma=False,
    )
```
